1024 devices in a mesh: row: 32 (over z_lo, core), col: 32 (over y, z_hi, x).
Axes of the slice: x: 4, y: 4, z: 32 (z_hi: 2, z_lo: 16; z = z_hi * 16 + z_lo), core: 2. Of those that a mesh axis runs over, the one named last changes fastest.
Arguments:
- left_blocks: float32 [32, 32, 8, 128, 128], P('row', 'col'), may hold values from -6 to 6
- left_rows: int32 [32, 32, 8], P('row', 'col'), may hold values from 0 to 7
- left_cols: int32 [32, 32, 8], P('row', 'col'), may hold values from 0 to 31
- left_count: int32 [32, 32], P('row', 'col'), may hold values from 4 to 8, as said below
- right_blocks: float32 [32, 32, 20, 128, 128], P('row', 'col'), may hold values from -0.5 to 0.5
- right_rows: int32 [32, 32, 20], P('row', 'col'), may hold values from 0 to 31, as said below
- right_cols: int32 [32, 32, 20], P('row', 'col'), may hold values from 0 to 31
- right_count: int32 [32, 32], P('row', 'col'), may hold values from 10 to 20, as said below
- out_rows: int32 [32, 32, 24], P('row', 'col'), may hold values from 0 to 7, as said below
- out_cols: int32 [32, 32, 24], P('row', 'col'), may hold values from 0 to 31
Outputs:
- product_blocks: float32 [32, 32, 24, 128, 128], P('row', 'col')
The draws below stay inside these ranges and needn't reach their ends.
Inputs may be any that keep to these rules, and one draw needn't show every extreme that they name: `left_count`: the live slots of one left list name distinct block rows and distinct inner indices; every left list has at least half of its 8 slots live and some list has all live. `right_rows`: the live slots of one right list name distinct positions, and at most 2 of them share an inner block index; the first two slots of every list share one. `right_count`: some right list has all 20 slots live. `out_rows`: the 24 product slots of one tile name distinct positions.
All inputs are finite; a program needn't handle non-finite values.
Results may differ from the reference program's by a relative error of at most 0.0003.
Values sent between devices are 32-bit elements; how exact they have to be, the bound alone decides.
No kernel may reach another device: no remote copies, remote signals or barrier semaphores. Data moves between devices by JAX's collectives and lax.ppermute only.
A program may use at most 32 MiB of HBM per device.

```python
import jax
import jax.numpy as jnp
from jax import lax

BS = 128
INB = 32
COLB = 32
ROWB = 8
MAXB = 20
STEPS = 3
MAXA = 8
CMAX = 24
N_ROW = 32
N_COL = 32


def shared_band(key):
    key = jax.random.fold_in(key, 404)
    inner = jax.random.permutation(key, INB - 2)[:MAXB // 2 - 2].astype(jnp.int32) + 1
    ends = jnp.array([0, INB - 1], dtype=jnp.int32)
    return jnp.concatenate([ends, inner])


def pattern_left(key):
    band = shared_band(key)
    key = jax.random.fold_in(key, 101)
    key_pos, key_rows, key_count, key_full = jax.random.split(key, 4)
    tiles = N_ROW * N_COL
    col_picks = jax.vmap(lambda k: jax.random.permutation(k, MAXB // 2)[:MAXA])(jax.random.split(key_pos, tiles)).astype(jnp.int32)
    cols = band[col_picks].reshape(N_ROW, N_COL, MAXA)
    rows = jax.vmap(lambda k: jax.random.permutation(k, ROWB)[:MAXA])(jax.random.split(key_rows, tiles)).astype(jnp.int32)
    rows = rows.reshape(N_ROW, N_COL, MAXA)
    counts = jax.random.randint(key_count, (tiles,), max(1, MAXA // 2), MAXA + 1)
    full = jax.random.randint(key_full, (), 0, tiles)
    counts = counts.at[full].set(MAXA).reshape(N_ROW, N_COL).astype(jnp.int32)
    return (rows, cols, counts)


def one_right(key, band):
    key_order, key_cols = jax.random.split(key, 2)
    order = jax.random.permutation(key_order, MAXB // 2).astype(jnp.int32)
    rows = jnp.repeat(band[order], 2)
    col_keys = jax.random.split(key_cols, MAXB // 2)
    cols = jax.vmap(lambda k: jax.random.permutation(k, COLB)[:2])(col_keys).astype(jnp.int32).reshape(-1)
    return (rows, cols)


def pattern_right(key):
    band = shared_band(key)
    key = jax.random.fold_in(key, 202)
    key_pos, key_count, key_full = jax.random.split(key, 3)
    tiles = N_ROW * N_COL
    rows, cols = jax.vmap(lambda k: one_right(k, band))(jax.random.split(key_pos, tiles))
    counts = jax.random.randint(key_count, (tiles,), max(2, MAXB // 2), MAXB + 1)
    full = jax.random.randint(key_full, (), 0, tiles)
    counts = counts.at[full].set(MAXB).reshape(N_ROW, N_COL).astype(jnp.int32)
    return (rows.reshape(N_ROW, N_COL, MAXB).astype(jnp.int32), cols.reshape(N_ROW, N_COL, MAXB).astype(jnp.int32), counts)


def pattern_out(key):
    left_rows, left_cols, left_count = pattern_left(key)
    right_rows, right_cols, right_count = pattern_right(key)
    left_live = (jnp.arange(MAXA, dtype=jnp.int32) < left_count[..., None]).astype(jnp.int32)
    right_live = (jnp.arange(MAXB, dtype=jnp.int32) < right_count[..., None]).astype(jnp.int32)
    left_mask = jnp.einsum('ijar,ijac->ijrc', jax.nn.one_hot(left_rows, ROWB, dtype=jnp.int32) * left_live[..., None], jax.nn.one_hot(left_cols, INB, dtype=jnp.int32))
    right_mask = jnp.einsum('ijbc,ijbq->ijcq', jax.nn.one_hot(right_rows, INB, dtype=jnp.int32) * right_live[..., None], jax.nn.one_hot(right_cols, COLB, dtype=jnp.int32))
    hits = jnp.zeros((N_ROW, N_COL, ROWB, COLB), jnp.int32)
    for offset in range(STEPS):
        hits = hits + jnp.einsum('ijrc,ijcq->ijrq', jnp.roll(left_mask, -offset, axis=1), jnp.roll(right_mask, -offset, axis=0))
    hit_flag = (hits > 0).astype(jnp.int32).reshape(N_ROW * N_COL, ROWB * COLB)
    key_rank = jax.random.fold_in(key, 303)
    ranks = jax.vmap(lambda k: jax.random.permutation(k, ROWB * COLB))(jax.random.split(key_rank, N_ROW * N_COL)).astype(jnp.int32)
    scores = hit_flag * (ROWB * COLB) + ranks
    top_scores, places = jax.lax.top_k(scores, CMAX)
    places = places.astype(jnp.int32)
    return ((places // COLB).reshape(N_ROW, N_COL, CMAX), (places % COLB).reshape(N_ROW, N_COL, CMAX))


def draw_left_rows(key, part):
    return pattern_left(key)[0]


def draw_left_cols(key, part):
    return pattern_left(key)[1]


def draw_left_count(key, part):
    return pattern_left(key)[2]


def draw_right_rows(key, part):
    return pattern_right(key)[0]


def draw_right_cols(key, part):
    return pattern_right(key)[1]


def draw_right_count(key, part):
    return pattern_right(key)[2]


def draw_out_rows(key, part):
    return pattern_out(key)[0]


def draw_out_cols(key, part):
    return pattern_out(key)[1]


def block_scale(own_key, shape, cuts, least, high):
    level, own = 1.0, jax.random.fold_in(own_key, 6)
    for position, shards_of in cuts:
        steps = jnp.exp(jax.random.uniform(jax.random.fold_in(own, position), (shards_of,), jnp.float32, least / len(cuts), high / len(cuts)))
        level = level * jnp.repeat(steps, shape[position] // shards_of).reshape([-1 if axis == position else 1 for axis in range(len(shape))])
    return level


def normal_values(own_key, extent, scale, bound, pieces=(), kind=jnp.bfloat16):
    values = jax.random.normal(own_key, extent, jnp.float32) * scale
    if len(pieces) > 0:
        values = block_scale(own_key, extent, pieces, -0.22, 0.18) * values
    return jnp.clip(values, min=-bound, max=bound).astype(kind)


def setup_inputs(seed: int = 0) -> dict:
    key_list = jax.random.split(jax.random.key(seed), 11)
    left_blocks = normal_values(key_list[0], (N_ROW, N_COL, MAXA, BS, BS), 1.0, 6.0, ((0, 32), (1, 32)), jnp.float32)
    left_rows = draw_left_rows(jax.random.fold_in(key_list[10], 71), 0)
    left_cols = draw_left_cols(jax.random.fold_in(key_list[10], 71), 0)
    left_count = draw_left_count(jax.random.fold_in(key_list[10], 71), 0)
    right_blocks = normal_values(key_list[4], (N_ROW, N_COL, MAXB, BS, BS), BS ** -0.5, 0.5, ((0, 32), (1, 32)), jnp.float32)
    right_rows = draw_right_rows(jax.random.fold_in(key_list[10], 71), 0)
    right_cols = draw_right_cols(jax.random.fold_in(key_list[10], 71), 0)
    right_count = draw_right_count(jax.random.fold_in(key_list[10], 71), 0)
    out_rows = draw_out_rows(jax.random.fold_in(key_list[10], 71), 0)
    out_cols = draw_out_cols(jax.random.fold_in(key_list[10], 71), 0)
    return dict(left_blocks=left_blocks, left_rows=left_rows, left_cols=left_cols, left_count=left_count, right_blocks=right_blocks, right_rows=right_rows, right_cols=right_cols, right_count=right_count, out_rows=out_rows, out_cols=out_cols)


def local_terms(left_blocks, left_rows, left_cols, left_count, right_blocks, right_rows, right_cols, right_count, out_rows, out_cols):
    left_live = jnp.arange(left_rows.shape[0], dtype=jnp.int32) < left_count
    right_live = jnp.arange(right_rows.shape[0], dtype=jnp.int32) < right_count
    matched = ((left_cols[:, None] == right_rows[None, :]) & left_live[:, None] & right_live[None, :]).astype(jnp.int32)
    ranking = jnp.cumsum(matched, axis=1) * matched
    chosen = jnp.stack([ranking == 1, ranking == 2], axis=1)
    positions = jnp.arange(right_rows.shape[0], dtype=jnp.int32)
    picks = jnp.sum(jnp.where(chosen, positions, 0), axis=2).astype(jnp.int32)
    present = jnp.any(chosen, axis=2)
    picked = right_blocks[picks]
    products = jnp.einsum("acd,amdf->amcf", left_blocks, picked, precision=lax.Precision.HIGHEST)
    pick_cols = right_cols[picks]
    weight = present[None] & (left_rows[None, :, None] == out_rows[:, None, None]) & (pick_cols[None] == out_cols[:, None, None])
    slots = out_rows.shape[0]
    block_size = left_blocks.shape[1]
    flat_weight = weight.astype(jnp.float32).reshape(slots, -1)
    flat_products = products.reshape(-1, block_size * block_size)
    summed = jnp.dot(flat_weight, flat_products, precision=lax.Precision.HIGHEST, preferred_element_type=jnp.float32)
    return summed.reshape(slots, block_size, block_size)


def reference(left_blocks, left_rows, left_cols, left_count, right_blocks, right_rows, right_cols, right_count, out_rows, out_cols):
    def per_row(row_index):
        running = jnp.zeros((N_COL, CMAX, BS, BS), jnp.float32)
        for offset in range(STEPS):
            source = (row_index + offset) % N_ROW
            running = running + jax.vmap(local_terms)(
                jnp.roll(left_blocks[row_index], -offset, axis=0),
                jnp.roll(left_rows[row_index], -offset, axis=0),
                jnp.roll(left_cols[row_index], -offset, axis=0),
                jnp.roll(left_count[row_index], -offset, axis=0),
                right_blocks[source], right_rows[source], right_cols[source], right_count[source],
                out_rows[row_index], out_cols[row_index])
        return running
    return lax.map(per_row, jnp.arange(N_ROW, dtype=jnp.int32))
```

```python
import jax
import jax.numpy as jnp
from jax import lax
from jax.experimental import pallas as pl
from jax.experimental.pallas import tpu as pltpu
from jax.sharding import PartitionSpec as P

BS = 128
MAXA = 8
MAXB = 20
CMAX = 24
ROWB = 8
INB = 32
COLB = 32
HALF = MAXA // 2 * BS
PAD = 8
LEFT_HALF = HALF + PAD
RIGHT_ROWS = MAXB * BS
N_ROW = 32
N_COL = 32
AXES = ("row", "col")

GROUP = 4
N_GROUP = N_COL // GROUP


def route(place):
    pairs = []
    for row in range(N_ROW):
        for col in range(N_COL):
            target = place(row, col // GROUP, col % GROUP)
            if target is not None:
                r, g, x = target
                pairs.append((row * N_COL + col, (r % N_ROW) * N_COL + (g % N_GROUP) * GROUP + x))
    return pairs


def along_x(moves):
    return route(lambda r, g, x: (r, g, moves[x]) if x in moves else None)


def to_previous_group(moves):
    return route(lambda r, g, x: (r, g - 1, moves[x]) if x in moves else None)


def send(block, pairs):
    return lax.ppermute(block, AXES, pairs)


def clear(table, size):
    def body(i, carry):
        table[i] = -1
        return carry

    lax.fori_loop(0, size, body, 0, unroll=8)


def mark_slots(out_rows, out_cols, slot_of):
    clear(slot_of, ROWB * COLB)
    for c in range(CMAX):
        slot_of[out_rows[c] * COLB + out_cols[c]] = c


def list_products(left_meta, right_meta, slot_of, by_inner, products, start):
    def left_int(i):
        return left_meta[0, i].astype(jnp.int32)

    def right_int(i):
        return right_meta[0, i].astype(jnp.int32)

    left_count = left_int(2 * MAXA)
    right_count = right_int(2 * MAXB)
    clear(by_inner, 2 * INB)
    for b in range(MAXB):
        place = jnp.where(b < right_count, right_int(b) * 2, 2 * INB)
        taken = (by_inner[place] >= 0) & (b < right_count)
        by_inner[place + taken.astype(jnp.int32)] = b
    count = start
    for a in range(MAXA):
        row, inner = left_int(a), left_int(MAXA + a)
        for m in range(2):
            b = by_inner[inner * 2 + m]
            column = right_int(MAXB + jnp.maximum(b, 0))
            c = slot_of[row * COLB + column]
            products[count] = (a * 32 + b) * 32 + c
            valid = (a < left_count) & (b >= 0) & (c >= 0)
            count = count + valid.astype(jnp.int32)
    return count


def split(value):
    high = value.astype(jnp.bfloat16)
    low = (value - high.astype(jnp.float32)).astype(jnp.bfloat16)
    return high, low


def multiply(products, first, last, left, right, total):
    def body(i, carry):
        code = products[i]
        a = code // 1024
        b = (code // 32) % 32
        c = code % 32
        left_high, left_low = split(left[pl.ds(pl.multiple_of(a * BS, BS), BS), :])
        right_high, right_low = split(right[pl.ds(pl.multiple_of(b * BS, BS), BS), :])
        lhs = jnp.concatenate([left_high, left_low], axis=1)
        both = jnp.concatenate([right_high, right_low], axis=1)
        rhs = jnp.concatenate([both, both], axis=0)
        pair = jnp.dot(lhs, rhs, preferred_element_type=jnp.float32)
        place = pl.ds(pl.multiple_of(c * BS, BS), BS)
        total[place, :] = total[place, :] + (pair[:, :BS] + pair[:, BS:])
        return carry

    lax.fori_loop(first, last, body, 0)


def first_kernel(
    out_rows, out_cols, left_hbm, right_hbm, out_hbm, left, right, total, left_meta, right_meta, slot_of, by_inner, products, sems
):
    copies = [
        pltpu.make_async_copy(left_hbm.at[pl.ds(HALF, PAD)], left_meta, sems.at[0]),
        pltpu.make_async_copy(right_hbm.at[pl.ds(RIGHT_ROWS, PAD)], right_meta, sems.at[1]),
        pltpu.make_async_copy(left_hbm.at[pl.ds(0, HALF)], left.at[pl.ds(0, HALF)], sems.at[2]),
        pltpu.make_async_copy(left_hbm.at[pl.ds(LEFT_HALF, HALF)], left.at[pl.ds(HALF, HALF)], sems.at[3]),
        pltpu.make_async_copy(right_hbm.at[pl.ds(0, RIGHT_ROWS)], right, sems.at[4]),
    ]
    for copy in copies:
        copy.start()
    mark_slots(out_rows, out_cols, slot_of)
    total[...] = jnp.zeros_like(total)
    copies[0].wait()
    copies[1].wait()
    count = list_products(left_meta, right_meta, slot_of, by_inner, products, 0)
    for copy in copies[2:]:
        copy.wait()
    multiply(products, 0, count, left, right, total)
    out = pltpu.make_async_copy(total, out_hbm, sems.at[0])
    out.start()
    out.wait()


def last_kernel(
    place, out_rows, out_cols, near, far, across_low, across_high, over_low, over_high, right_core, right_next, right_both, total_hbm, out_hbm,
    left, right, total, left_meta, right_meta, slot_of, by_inner, products, sems,
):
    x, core = place[0], place[1]

    def left_copies(step, low, low_at, high, high_at):
        base = step * MAXA * BS
        return [
            pltpu.make_async_copy(low.at[pl.ds(low_at + HALF, PAD)], left_meta.at[step], sems.at[step, 0]),
            pltpu.make_async_copy(low.at[pl.ds(low_at, HALF)], left.at[pl.ds(base, HALF)], sems.at[step, 1]),
            pltpu.make_async_copy(high.at[pl.ds(high_at, HALF)], left.at[pl.ds(base + HALF, HALF)], sems.at[step, 2]),
        ]

    def right_copies(step, source):
        return [
            pltpu.make_async_copy(source.at[pl.ds(RIGHT_ROWS, PAD)], right_meta.at[step], sems.at[step, 3]),
            pltpu.make_async_copy(
                source.at[pl.ds(0, RIGHT_ROWS)], right.at[pl.ds(step * RIGHT_ROWS, RIGHT_ROWS)], sems.at[step, 4]
            ),
        ]

    def start(copies):
        for copy in copies:
            copy.start()

    base_copy = pltpu.make_async_copy(total_hbm, total, sems.at[2, 0])
    one_left = left_copies(0, over_low, 0, over_high, 0)
    two_left = left_copies(1, across_low, 0, across_high, 0)
    one_right = right_copies(0, right_core)
    two_right = right_copies(1, right_next)

    pl.when(x < 3)(lambda: start(left_copies(0, near, 0, near, LEFT_HALF)))
    pl.when(x == 3)(lambda: start(one_left))
    pl.when(core == 0)(lambda: start(one_right))
    pl.when(core == 1)(lambda: start(right_copies(0, right_both)))
    base_copy.start()
    pl.when(x < 2)(lambda: start(left_copies(1, far, 0, far, LEFT_HALF)))
    pl.when(x >= 2)(lambda: start(two_left))
    start(two_right)

    mark_slots(out_rows, out_cols, slot_of)
    one_left[0].wait()
    one_right[0].wait()
    middle = list_products(left_meta.at[0], right_meta.at[0], slot_of, by_inner, products, 0)
    two_left[0].wait()
    two_right[0].wait()
    end = list_products(left_meta.at[1], right_meta.at[1], slot_of, by_inner, products, middle)
    base_copy.wait()
    for copy in one_left[1:] + one_right[1:]:
        copy.wait()
    multiply(products, 0, middle, left, right, total)
    for copy in two_left[1:] + two_right[1:]:
        copy.wait()
    multiply(
        products, middle, end, left.at[pl.ds(MAXA * BS, MAXA * BS)], right.at[pl.ds(RIGHT_ROWS, RIGHT_ROWS)], total
    )
    out = pltpu.make_async_copy(total, out_hbm, sems.at[2, 1])
    out.start()
    out.wait()


SMEM_SPEC = pl.BlockSpec(memory_space=pltpu.SMEM)
ANY_SPEC = pl.BlockSpec(memory_space=pl.ANY)


def tables():
    return [
        pltpu.SMEM((ROWB * COLB,), jnp.int32),
        pltpu.SMEM((2 * INB + 8,), jnp.int32),
        pltpu.SMEM((64,), jnp.int32),
    ]


def first_step(out_rows, out_cols, left, right):
    return pl.pallas_call(
        first_kernel,
        out_shape=jax.ShapeDtypeStruct((CMAX * BS, BS), jnp.float32),
        in_specs=[SMEM_SPEC] * 2 + [ANY_SPEC] * 2,
        out_specs=ANY_SPEC,
        scratch_shapes=[
            pltpu.VMEM((MAXA * BS, BS), jnp.float32),
            pltpu.VMEM((RIGHT_ROWS, BS), jnp.float32),
            pltpu.VMEM((CMAX * BS, BS), jnp.float32),
            pltpu.SMEM((PAD, BS), jnp.float32),
            pltpu.SMEM((PAD, BS), jnp.float32),
        ]
        + tables()
        + [pltpu.SemaphoreType.DMA((5,))],
        compiler_params=pltpu.CompilerParams(vmem_limit_bytes=16 * 2**20),
        name="first_step",
    )(out_rows, out_cols, left, right)


def last_steps(place, out_rows, out_cols, buffers, total):
    return pl.pallas_call(
        last_kernel,
        out_shape=jax.ShapeDtypeStruct((CMAX * BS, BS), jnp.float32),
        in_specs=[SMEM_SPEC] * 3 + [ANY_SPEC] * (len(buffers) + 1),
        out_specs=ANY_SPEC,
        input_output_aliases={3 + len(buffers): 0},
        scratch_shapes=[
            pltpu.VMEM((2 * MAXA * BS, BS), jnp.float32),
            pltpu.VMEM((2 * RIGHT_ROWS, BS), jnp.float32),
            pltpu.VMEM((CMAX * BS, BS), jnp.float32),
            pltpu.SMEM((2, PAD, BS), jnp.float32),
            pltpu.SMEM((2, PAD, BS), jnp.float32),
        ]
        + tables()
        + [pltpu.SemaphoreType.DMA((3, 5))],
        compiler_params=pltpu.CompilerParams(vmem_limit_bytes=16 * 2**20),
        name="last_steps",
    )(place, out_rows, out_cols, *buffers, total)


def meta_rows(*parts):
    line = jnp.concatenate(parts).astype(jnp.float32)
    return jnp.pad(line[None], ((0, PAD - 1), (0, BS - line.shape[0])))


def shards(
    left_blocks,
    left_rows,
    left_cols,
    left_count,
    right_blocks,
    right_rows,
    right_cols,
    right_count,
    out_rows,
    out_cols,
):
    left_meta = meta_rows(left_rows[0, 0], left_cols[0, 0], left_count[0])
    right_meta = meta_rows(right_rows[0, 0], right_cols[0, 0], right_count[0])
    blocks = left_blocks.reshape(MAXA * BS, BS)
    low = jnp.concatenate([blocks[:HALF], left_meta])
    high = jnp.concatenate([blocks[HALF:], left_meta])
    left = jnp.concatenate([low, high])
    right = jnp.concatenate([right_blocks.reshape(RIGHT_ROWS, BS), right_meta])
    place = jnp.stack([lax.axis_index("col") % GROUP, lax.axis_index("row") % 2]).astype(jnp.int32)

    spread = send(high, along_x({0: 3, 1: 2}))
    across_low = send(low, to_previous_group({0: 2, 1: 3}))
    right_next = send(right, route(lambda r, g, x: (r - 2, g, x)))
    near = send(left, along_x({1: 0, 2: 1, 3: 2}))
    far = send(left, along_x({2: 0, 3: 1}))
    across_high = send(spread, to_previous_group({3: 2, 2: 3}))
    left, right, _ = lax.optimization_barrier((left, right, spread))
    total = first_step(out_rows[0, 0], out_cols[0, 0], left, right)
    right, total, near, far, across_low, across_high = lax.optimization_barrier(
        (right, total, near, far, across_low, across_high)
    )
    over_low = send(across_low, along_x({2: 3}))
    over_high = send(across_high, along_x({2: 3}))
    right_core = send(right, route(lambda r, g, x: (r - 1, g, x) if r % 2 else None))
    right_next, right_core, over_low, over_high = lax.optimization_barrier(
        (right_next, right_core, over_low, over_high)
    )
    right_both = send(right_next, route(lambda r, g, x: (r + 1, g, x) if r % 2 == 0 else None))
    buffers = [near, far, across_low, across_high, over_low, over_high, right_core, right_next, right_both]
    total = last_steps(place, out_rows[0, 0], out_cols[0, 0], buffers, total)
    return total.reshape(1, 1, CMAX, BS, BS)


def solution(mesh):
    in_specs = (
        P("row", "col", None, None, None),
        P("row", "col", None),
        P("row", "col", None),
        P("row", "col"),
        P("row", "col", None, None, None),
        P("row", "col", None),
        P("row", "col", None),
        P("row", "col"),
        P("row", "col", None),
        P("row", "col", None),
    )
    out_specs = P("row", "col", None, None, None)
    return jax.shard_map(shards, mesh=mesh, in_specs=in_specs, out_specs=out_specs, check_vma=False)
```

```python
import functools

import jax
import jax.numpy as jnp
from jax import lax
from jax.experimental import pallas as pl
from jax.experimental.pallas import tpu as pltpu
from jax.sharding import PartitionSpec as P

BS = 128
MAXA = 8
MAXB = 20
CMAX = 24
ROWB = 8
INB = 32
COLB = 32
HALF = MAXA // 2 * BS
PAD = 8
LEFT_HALF = HALF + PAD
RIGHT_ROWS = MAXB * BS
N_ROW = 32
N_COL = 32
AXES = ("row", "col")

GROUP = 4
N_GROUP = N_COL // GROUP


def route(place):
    pairs = []
    for row in range(N_ROW):
        for col in range(N_COL):
            target = place(row, col // GROUP, col % GROUP)
            if target is not None:
                r, g, x = target
                pairs.append((row * N_COL + col, (r % N_ROW) * N_COL + (g % N_GROUP) * GROUP + x))
    return pairs


def along_x(moves):
    return route(lambda r, g, x: (r, g, moves[x]) if x in moves else None)


def to_previous_group(moves):
    return route(lambda r, g, x: (r, g - 1, moves[x]) if x in moves else None)


def send(block, pairs):
    return lax.ppermute(block, AXES, pairs)


def clear(table, size):
    def body(i, carry):
        table[i] = -1
        return carry

    lax.fori_loop(0, size, body, 0, unroll=8)


def mark_slots(out_rows, out_cols, slot_of):
    clear(slot_of, ROWB * COLB)
    for c in range(CMAX):
        slot_of[out_rows[c] * COLB + out_cols[c]] = c


def list_products(left_meta, right_meta, slot_of, by_inner, products, start):
    def left_int(i):
        return left_meta[0, i].astype(jnp.int32)

    def right_int(i):
        return right_meta[0, i].astype(jnp.int32)

    left_count = left_int(2 * MAXA)
    right_count = right_int(2 * MAXB)
    clear(by_inner, 2 * INB)
    for b in range(MAXB):
        place = jnp.where(b < right_count, right_int(b) * 2, 2 * INB)
        taken = (by_inner[place] >= 0) & (b < right_count)
        by_inner[place + taken.astype(jnp.int32)] = b
    count = start
    for a in range(MAXA):
        row, inner = left_int(a), left_int(MAXA + a)
        for m in range(2):
            b = by_inner[inner * 2 + m]
            column = right_int(MAXB + jnp.maximum(b, 0))
            c = slot_of[row * COLB + column]
            products[count] = (a * 32 + b) * 32 + c
            valid = (a < left_count) & (b >= 0) & (c >= 0)
            count = count + valid.astype(jnp.int32)
    return count


def split(value):
    high = value.astype(jnp.bfloat16)
    low = (value - high.astype(jnp.float32)).astype(jnp.bfloat16)
    return high, low


def step_kernel(picks, n_left, n_right, first, *refs):
    sides, out_rows, out_cols = refs[:3]
    lefts = refs[3 : 3 + n_left]
    rights = refs[3 + n_left : 3 + n_left + n_right]
    (total, left_tile, right_tile, left_meta, right_meta, slot_of, by_inner, products, sems) = refs[-9:]
    other_left, other_right = sides[0] == 1, sides[1] == 1

    def left_at(pick, sem):
        return pltpu.make_async_copy(lefts[pick[0]].at[pl.ds(pick[1] + HALF, PAD)], left_meta, sem)

    def right_at(ref, sem):
        return pltpu.make_async_copy(ref.at[pl.ds(RIGHT_ROWS, PAD)], right_meta, sem)

    def either(condition, same, no, yes):
        if same:
            no()
        else:
            pl.when(condition)(yes)
            pl.when(jnp.logical_not(condition))(no)

    either(
        other_left,
        picks[0][0] == picks[1][0],
        lambda: left_at(picks[0][0], sems.at[0]).start(),
        lambda: left_at(picks[1][0], sems.at[0]).start(),
    )
    either(
        other_right,
        n_right == 1,
        lambda: right_at(rights[0], sems.at[1]).start(),
        lambda: right_at(rights[-1], sems.at[1]).start(),
    )
    mark_slots(out_rows, out_cols, slot_of)
    total[...] = jnp.zeros_like(total) if first else refs[3 + n_left + n_right][...]
    left_at(picks[0][0], sems.at[0]).wait()
    right_at(rights[0], sems.at[1]).wait()
    count = list_products(left_meta, right_meta, slot_of, by_inner, products, 0)

    def copy_tile(tile, ref, start):
        tile[...] = ref[pl.ds(pl.multiple_of(start, 8), BS), :]

    def copy_half(pick, start):
        copy_tile(left_tile, lefts[pick[0]], pick[1] + start)

    def body(i, carry):
        code = products[i]
        a = code // 1024
        b = (code // 32) % 32
        c = code % 32
        upper = a // (MAXA // 2)
        at = (a % (MAXA // 2)) * BS
        for half in range(2):

            @pl.when(upper == half)
            def _():
                one, other = picks[0][half], picks[1][half]
                either(other_left, one == other, lambda: copy_half(one, at), lambda: copy_half(other, at))

        either(
            other_right,
            n_right == 1,
            lambda: copy_tile(right_tile, rights[0], b * BS),
            lambda: copy_tile(right_tile, rights[-1], b * BS),
        )
        left_high_part, left_low_part = split(left_tile[...])
        right_high_part, right_low_part = split(right_tile[...])
        lhs = jnp.concatenate([left_high_part, left_low_part], axis=1)
        both = jnp.concatenate([right_high_part, right_low_part], axis=1)
        rhs = jnp.concatenate([both, both], axis=0)
        pair = jnp.dot(lhs, rhs, preferred_element_type=jnp.float32)
        place = pl.ds(pl.multiple_of(c * BS, BS), BS)
        total[place, :] = total[place, :] + (pair[:, :BS] + pair[:, BS:])
        return carry

    lax.fori_loop(0, count, body, 0)


WHOLE = ((0, 0), (0, LEFT_HALF))
SMEM_SPEC = pl.BlockSpec(memory_space=pltpu.SMEM)
VMEM_SPEC = pl.BlockSpec(memory_space=pltpu.VMEM)


def step_call(name, sides, out_rows, out_cols, lefts, picks, rights, before=None):
    operands = [sides, out_rows, out_cols, *lefts, *rights] + ([] if before is None else [before])
    return pl.pallas_call(
        functools.partial(step_kernel, picks, len(lefts), len(rights), before is None),
        out_shape=jax.ShapeDtypeStruct((CMAX * BS, BS), jnp.float32),
        in_specs=[SMEM_SPEC] * 3 + [VMEM_SPEC] * (len(operands) - 3),
        out_specs=VMEM_SPEC,
        input_output_aliases={} if before is None else {len(operands) - 1: 0},
        scratch_shapes=[
            pltpu.VMEM((BS, BS), jnp.float32),
            pltpu.VMEM((BS, BS), jnp.float32),
            pltpu.SMEM((PAD, BS), jnp.float32),
            pltpu.SMEM((PAD, BS), jnp.float32),
            pltpu.SMEM((ROWB * COLB,), jnp.int32),
            pltpu.SMEM((2 * INB + 8,), jnp.int32),
            pltpu.SMEM((32,), jnp.int32),
            pltpu.SemaphoreType.DMA((2,)),
        ],
        compiler_params=pltpu.CompilerParams(vmem_limit_bytes=24 * 2**20),
        cost_estimate=pl.CostEstimate(flops=10**10 if before is None else 10**8, bytes_accessed=10**6, transcendentals=0),
        name=name,
    )(*operands)


def meta_rows(*parts):
    line = jnp.concatenate(parts).astype(jnp.float32)
    return jnp.pad(line[None], ((0, PAD - 1), (0, BS - line.shape[0])))


def shards(
    left_blocks,
    left_rows,
    left_cols,
    left_count,
    right_blocks,
    right_rows,
    right_cols,
    right_count,
    out_rows,
    out_cols,
):
    left_meta = meta_rows(left_rows[0, 0], left_cols[0, 0], left_count[0])
    right_meta = meta_rows(right_rows[0, 0], right_cols[0, 0], right_count[0])
    blocks = left_blocks.reshape(MAXA * BS, BS)
    low = jnp.concatenate([blocks[:HALF], left_meta])
    high = jnp.concatenate([blocks[HALF:], left_meta])
    left = jnp.concatenate([low, high])
    right = jnp.concatenate([right_blocks.reshape(RIGHT_ROWS, BS), right_meta])
    x = lax.axis_index("col") % GROUP
    row = lax.axis_index("row")
    core = row % 2
    last_chip = (row // 2 == N_ROW // 2 - 1).astype(jnp.int32)
    rows, cols = out_rows[0, 0], out_cols[0, 0]

    right_near = send(right, route(lambda r, g, x: (r - 2, g, x) if r >= 2 else None))
    high_far = send(high, along_x({0: 3, 1: 2, 2: 0, 3: 1}))
    low_far = send(low, route(lambda r, g, x: (r, g - 1, x + 2) if x < 2 else (r, g, x - 2)))
    near = send(left, along_x({1: 0, 2: 1, 3: 2}))
    across_high = send(high_far, to_previous_group({3: 2, 2: 3}))
    left, right, high_far = lax.optimization_barrier((left, right, high_far))
    right_wrap = send(right, route(lambda r, g, x: (r - 2, g, x) if r < 2 else None))
    total = step_call("step_0", jnp.zeros((2,), jnp.int32), rows, cols, [left], (WHOLE, WHOLE), [right])
    right, near, total, low_far = lax.optimization_barrier((right, near, total, low_far))
    across_high, total = lax.optimization_barrier((across_high, total))
    over_low = send(low_far, along_x({2: 3}))
    over_high = send(across_high, along_x({2: 3}))

    right_one = send(
        lax.select(core == 1, right, right_near),
        route(lambda r, g, x: (r ^ 1, g, x)),
    )
    right_wrap, over_low, over_high = lax.optimization_barrier((right_wrap, over_low, over_high))
    edge = send(right_wrap, route(lambda r, g, x: (r + 1, g, x) if r == N_ROW - 2 else None))
    total = step_call(
        "step_2",
        jnp.stack([(x >= 2).astype(jnp.int32), last_chip]),
        rows,
        cols,
        [low_far, high_far, across_high],
        (((0, 0), (1, 0)), ((0, 0), (2, 0))),
        [right_near, right_wrap],
        total,
    )
    total = step_call(
        "step_1",
        jnp.stack([(x == 3).astype(jnp.int32), last_chip * core]),
        rows,
        cols,
        [near, over_low, over_high],
        (WHOLE, ((1, 0), (2, 0))),
        [right_one, edge],
        total,
    )
    return total.reshape(1, 1, CMAX, BS, BS)


def solution(mesh):
    in_specs = (
        P("row", "col", None, None, None),
        P("row", "col", None),
        P("row", "col", None),
        P("row", "col"),
        P("row", "col", None, None, None),
        P("row", "col", None),
        P("row", "col", None),
        P("row", "col"),
        P("row", "col", None),
        P("row", "col", None),
    )
    out_specs = P("row", "col", None, None, None)
    return jax.shard_map(shards, mesh=mesh, in_specs=in_specs, out_specs=out_specs, check_vma=False)
```

```python
import functools

import jax
import jax.numpy as jnp
from jax import lax
from jax.experimental import pallas as pl
from jax.experimental.pallas import tpu as pltpu
from jax.sharding import PartitionSpec as P

BS = 128
MAXA = 8
MAXB = 20
CMAX = 24
ROWB = 8
INB = 32
COLB = 32
HALF = MAXA // 2 * BS
PAD = 8
LEFT_HALF = HALF + PAD
RIGHT_ROWS = MAXB * BS
N_ROW = 32
N_COL = 32
AXES = ("row", "col")

GROUP = 4
N_GROUP = N_COL // GROUP


def route(place):
    pairs = []
    for row in range(N_ROW):
        for col in range(N_COL):
            target = place(row, col // GROUP, col % GROUP)
            if target is not None:
                r, g, x = target
                pairs.append((row * N_COL + col, (r % N_ROW) * N_COL + (g % N_GROUP) * GROUP + x))
    return pairs


def along_x(moves):
    return route(lambda r, g, x: (r, g, moves[x]) if x in moves else None)


def to_previous_group(moves):
    return route(lambda r, g, x: (r, g - 1, moves[x]) if x in moves else None)


def send(block, pairs):
    return lax.ppermute(block, AXES, pairs)


def clear(table, size):
    def body(i, carry):
        table[i] = -1
        return carry

    lax.fori_loop(0, size, body, 0, unroll=8)


def mark_slots(out_rows, out_cols, slot_of):
    clear(slot_of, ROWB * COLB)
    for c in range(CMAX):
        slot_of[out_rows[c] * COLB + out_cols[c]] = c


def list_products(left_meta, right_meta, slot_of, by_inner, products, start):
    def left_int(i):
        return left_meta[0, i].astype(jnp.int32)

    def right_int(i):
        return right_meta[0, i].astype(jnp.int32)

    left_count = left_int(2 * MAXA)
    right_count = right_int(2 * MAXB)
    clear(by_inner, 2 * INB)
    for b in range(MAXB):
        place = jnp.where(b < right_count, right_int(b) * 2, 2 * INB)
        taken = (by_inner[place] >= 0) & (b < right_count)
        by_inner[place + taken.astype(jnp.int32)] = b
    count = start
    for a in range(MAXA):
        row, inner = left_int(a), left_int(MAXA + a)
        for m in range(2):
            b = by_inner[inner * 2 + m]
            column = right_int(MAXB + jnp.maximum(b, 0))
            c = slot_of[row * COLB + column]
            products[count] = (a * 32 + b) * 32 + c
            valid = (a < left_count) & (b >= 0) & (c >= 0)
            count = count + valid.astype(jnp.int32)
    return count


def split(value):
    high = value.astype(jnp.bfloat16)
    low = (value - high.astype(jnp.float32)).astype(jnp.bfloat16)
    return high, low


def step_kernel(picks, n_left, n_right, first, *refs):
    sides, out_rows, out_cols = refs[:3]
    lefts = refs[3 : 3 + n_left]
    rights = refs[3 + n_left : 3 + n_left + n_right]
    (total, left_tile, right_tile, left_meta, right_meta, slot_of, by_inner, products, sems) = refs[-9:]
    other_left, other_right = sides[0] == 1, sides[1] == 1

    def left_at(pick, sem):
        return pltpu.make_async_copy(lefts[pick[0]].at[pl.ds(pick[1] + HALF, PAD)], left_meta, sem)

    def right_at(ref, sem):
        return pltpu.make_async_copy(ref.at[pl.ds(RIGHT_ROWS, PAD)], right_meta, sem)

    def either(condition, same, no, yes):
        if same:
            no()
        else:
            pl.when(condition)(yes)
            pl.when(jnp.logical_not(condition))(no)

    either(
        other_left,
        picks[0][0] == picks[1][0],
        lambda: left_at(picks[0][0], sems.at[0]).start(),
        lambda: left_at(picks[1][0], sems.at[0]).start(),
    )
    either(
        other_right,
        n_right == 1,
        lambda: right_at(rights[0], sems.at[1]).start(),
        lambda: right_at(rights[-1], sems.at[1]).start(),
    )
    mark_slots(out_rows, out_cols, slot_of)
    total[...] = jnp.zeros_like(total) if first else refs[3 + n_left + n_right][...]
    left_at(picks[0][0], sems.at[0]).wait()
    right_at(rights[0], sems.at[1]).wait()
    count = list_products(left_meta, right_meta, slot_of, by_inner, products, 0)

    def copy_tile(tile, ref, start):
        tile[...] = ref[pl.ds(pl.multiple_of(start, 8), BS), :]

    def copy_half(pick, start):
        copy_tile(left_tile, lefts[pick[0]], pick[1] + start)

    def body(i, carry):
        code = products[i]
        a = code // 1024
        b = (code // 32) % 32
        c = code % 32
        upper = a // (MAXA // 2)
        at = (a % (MAXA // 2)) * BS
        for half in range(2):

            @pl.when(upper == half)
            def _():
                one, other = picks[0][half], picks[1][half]
                either(other_left, one == other, lambda: copy_half(one, at), lambda: copy_half(other, at))

        either(
            other_right,
            n_right == 1,
            lambda: copy_tile(right_tile, rights[0], b * BS),
            lambda: copy_tile(right_tile, rights[-1], b * BS),
        )
        left_high_part, left_low_part = split(left_tile[...])
        right_high_part, right_low_part = split(right_tile[...])
        lhs = jnp.concatenate([left_high_part, left_low_part], axis=1)
        both = jnp.concatenate([right_high_part, right_low_part], axis=1)
        rhs = jnp.concatenate([both, both], axis=0)
        pair = jnp.dot(lhs, rhs, preferred_element_type=jnp.float32)
        place = pl.ds(pl.multiple_of(c * BS, BS), BS)
        total[place, :] = total[place, :] + (pair[:, :BS] + pair[:, BS:])
        return carry

    lax.fori_loop(0, count, body, 0)


WHOLE = ((0, 0), (0, LEFT_HALF))
SMEM_SPEC = pl.BlockSpec(memory_space=pltpu.SMEM)
VMEM_SPEC = pl.BlockSpec(memory_space=pltpu.VMEM)


def step_call(name, sides, out_rows, out_cols, lefts, picks, rights, before=None, flops=10**8):
    operands = [sides, out_rows, out_cols, *lefts, *rights] + ([] if before is None else [before])
    return pl.pallas_call(
        functools.partial(step_kernel, picks, len(lefts), len(rights), before is None),
        out_shape=jax.ShapeDtypeStruct((CMAX * BS, BS), jnp.float32),
        in_specs=[SMEM_SPEC] * 3 + [VMEM_SPEC] * (len(operands) - 3),
        out_specs=VMEM_SPEC,
        input_output_aliases={} if before is None else {len(operands) - 1: 0},
        scratch_shapes=[
            pltpu.VMEM((BS, BS), jnp.float32),
            pltpu.VMEM((BS, BS), jnp.float32),
            pltpu.SMEM((PAD, BS), jnp.float32),
            pltpu.SMEM((PAD, BS), jnp.float32),
            pltpu.SMEM((ROWB * COLB,), jnp.int32),
            pltpu.SMEM((2 * INB + 8,), jnp.int32),
            pltpu.SMEM((32,), jnp.int32),
            pltpu.SemaphoreType.DMA((2,)),
        ],
        compiler_params=pltpu.CompilerParams(vmem_limit_bytes=24 * 2**20),
        cost_estimate=pl.CostEstimate(flops=flops, bytes_accessed=10**6, transcendentals=0),
        name=name,
    )(*operands)


def meta_rows(*parts):
    line = jnp.concatenate(parts).astype(jnp.float32)
    return jnp.pad(line[None], ((0, PAD - 1), (0, BS - line.shape[0])))


def shards(
    left_blocks,
    left_rows,
    left_cols,
    left_count,
    right_blocks,
    right_rows,
    right_cols,
    right_count,
    out_rows,
    out_cols,
):
    left_meta = meta_rows(left_rows[0, 0], left_cols[0, 0], left_count[0])
    right_meta = meta_rows(right_rows[0, 0], right_cols[0, 0], right_count[0])
    blocks = left_blocks.reshape(MAXA * BS, BS)
    low = jnp.concatenate([blocks[:HALF], left_meta])
    high = jnp.concatenate([blocks[HALF:], left_meta])
    left = jnp.concatenate([low, high])
    right = jnp.concatenate([right_blocks.reshape(RIGHT_ROWS, BS), right_meta])
    x = lax.axis_index("col") % GROUP
    row = lax.axis_index("row")
    core = row % 2
    last_chip = (row // 2 == N_ROW // 2 - 1).astype(jnp.int32)
    rows, cols = out_rows[0, 0], out_cols[0, 0]

    high_far = send(high, along_x({0: 3, 1: 2, 2: 0, 3: 1}))
    right_near = send(right, route(lambda r, g, x: (r - 2, g, x) if r >= 2 else None))
    near = send(left, along_x({1: 0, 2: 1, 3: 2}))
    low_far = send(low, route(lambda r, g, x: (r, g - 1, x + 2) if x < 2 else (r, g, x - 2)))
    across_high = send(high_far, to_previous_group({3: 2, 2: 3}))
    left, right, high_far = lax.optimization_barrier((left, right, high_far))
    right_wrap = send(right, route(lambda r, g, x: (r - 2, g, x) if r < 2 else None))
    near, low_far = lax.optimization_barrier((near, low_far))
    over_low = send(low_far, along_x({2: 3}))
    left, across_high, low_far = lax.optimization_barrier((left, across_high, low_far))
    over_high = send(across_high, along_x({2: 3}))
    total = step_call("step_0", jnp.zeros((2,), jnp.int32), rows, cols, [left], (WHOLE, WHOLE), [right], flops=10000000000)
    right_near, total = lax.optimization_barrier((right_near, total))
    right_one = send(
        lax.select(core == 1, right, right_near),
        route(lambda r, g, x: (r ^ 1, g, x)),
    )
    right_wrap, over_low, over_high, total = lax.optimization_barrier((right_wrap, over_low, over_high, total))
    edge = send(right_wrap, route(lambda r, g, x: (r + 1, g, x) if r == N_ROW - 2 else None))
    total = step_call(
        "step_2",
        jnp.stack([(x >= 2).astype(jnp.int32), last_chip]),
        rows,
        cols,
        [low_far, high_far, across_high],
        (((0, 0), (1, 0)), ((0, 0), (2, 0))),
        [right_near, right_wrap],
        total,
    )
    total = step_call(
        "step_1",
        jnp.stack([(x == 3).astype(jnp.int32), last_chip * core]),
        rows,
        cols,
        [near, over_low, over_high],
        (WHOLE, ((1, 0), (2, 0))),
        [right_one, edge],
        total,
    )
    return total.reshape(1, 1, CMAX, BS, BS)


def solution(mesh):
    in_specs = (
        P("row", "col", None, None, None),
        P("row", "col", None),
        P("row", "col", None),
        P("row", "col"),
        P("row", "col", None, None, None),
        P("row", "col", None),
        P("row", "col", None),
        P("row", "col"),
        P("row", "col", None),
        P("row", "col", None),
    )
    out_specs = P("row", "col", None, None, None)
    return jax.shard_map(shards, mesh=mesh, in_specs=in_specs, out_specs=out_specs, check_vma=False)
```

```python
import functools

import jax
import jax.numpy as jnp
from jax import lax
from jax.experimental import pallas as pl
from jax.experimental.pallas import tpu as pltpu
from jax.sharding import PartitionSpec as P

BS = 128
MAXA = 8
MAXB = 20
CMAX = 24
ROWB = 8
INB = 32
COLB = 32
HALF = MAXA // 2 * BS
PAD = 8
LEFT_HALF = HALF + PAD
RIGHT_ROWS = MAXB * BS
N_ROW = 32
N_COL = 32
AXES = ("row", "col")

GROUP = 4
N_GROUP = N_COL // GROUP


def route(place):
    pairs = []
    for row in range(N_ROW):
        for col in range(N_COL):
            target = place(row, col // GROUP, col % GROUP)
            if target is not None:
                r, g, x = target
                pairs.append((row * N_COL + col, (r % N_ROW) * N_COL + (g % N_GROUP) * GROUP + x))
    return pairs


def along_x(moves):
    return route(lambda r, g, x: (r, g, moves[x]) if x in moves else None)


def to_previous_group(moves):
    return route(lambda r, g, x: (r, g - 1, moves[x]) if x in moves else None)


def send(block, pairs):
    return lax.ppermute(block, AXES, pairs)


def clear(table, size):
    def body(i, carry):
        table[i] = -1
        return carry

    lax.fori_loop(0, size, body, 0, unroll=8)


def mark_slots(out_rows, out_cols, slot_of):
    clear(slot_of, ROWB * COLB)
    for c in range(CMAX):
        slot_of[out_rows[c] * COLB + out_cols[c]] = c


def list_products(left_meta, right_meta, slot_of, by_inner, products, start):
    def left_int(i):
        return left_meta[0, i].astype(jnp.int32)

    def right_int(i):
        return right_meta[0, i].astype(jnp.int32)

    left_count = left_int(2 * MAXA)
    right_count = right_int(2 * MAXB)
    clear(by_inner, 2 * INB)
    for b in range(MAXB):
        place = jnp.where(b < right_count, right_int(b) * 2, 2 * INB)
        taken = (by_inner[place] >= 0) & (b < right_count)
        by_inner[place + taken.astype(jnp.int32)] = b
    count = start
    for a in range(MAXA):
        row, inner = left_int(a), left_int(MAXA + a)
        for m in range(2):
            b = by_inner[inner * 2 + m]
            column = right_int(MAXB + jnp.maximum(b, 0))
            c = slot_of[row * COLB + column]
            products[count] = (a * 32 + b) * 32 + c
            valid = (a < left_count) & (b >= 0) & (c >= 0)
            count = count + valid.astype(jnp.int32)
    return count


def split(value):
    high = value.astype(jnp.bfloat16)
    low = (value - high.astype(jnp.float32)).astype(jnp.bfloat16)
    return high, low


def step_kernel(picks, n_left, n_right, first, *refs):
    sides, out_rows, out_cols = refs[:3]
    lefts = refs[3 : 3 + n_left]
    rights = refs[3 + n_left : 3 + n_left + n_right]
    (total, left_tile, right_tile, left_meta, right_meta, slot_of, by_inner, products, sems) = refs[-9:]
    other_left, other_right = sides[0] == 1, sides[1] == 1

    def left_at(pick, sem):
        return pltpu.make_async_copy(lefts[pick[0]].at[pl.ds(pick[1] + HALF, PAD)], left_meta, sem)

    def right_at(ref, sem):
        return pltpu.make_async_copy(ref.at[pl.ds(RIGHT_ROWS, PAD)], right_meta, sem)

    def either(condition, same, no, yes):
        if same:
            no()
        else:
            pl.when(condition)(yes)
            pl.when(jnp.logical_not(condition))(no)

    either(
        other_left,
        picks[0][0] == picks[1][0],
        lambda: left_at(picks[0][0], sems.at[0]).start(),
        lambda: left_at(picks[1][0], sems.at[0]).start(),
    )
    either(
        other_right,
        n_right == 1,
        lambda: right_at(rights[0], sems.at[1]).start(),
        lambda: right_at(rights[-1], sems.at[1]).start(),
    )
    mark_slots(out_rows, out_cols, slot_of)
    total[...] = jnp.zeros_like(total) if first else refs[3 + n_left + n_right][...]
    left_at(picks[0][0], sems.at[0]).wait()
    right_at(rights[0], sems.at[1]).wait()
    count = list_products(left_meta, right_meta, slot_of, by_inner, products, 0)

    def copy_tile(tile, ref, start):
        tile[...] = ref[pl.ds(pl.multiple_of(start, 8), BS), :]

    def copy_half(pick, start):
        copy_tile(left_tile, lefts[pick[0]], pick[1] + start)

    def body(i, carry):
        code = products[i]
        a = code // 1024
        b = (code // 32) % 32
        c = code % 32
        upper = a // (MAXA // 2)
        at = (a % (MAXA // 2)) * BS
        for half in range(2):

            @pl.when(upper == half)
            def _():
                one, other = picks[0][half], picks[1][half]
                either(other_left, one == other, lambda: copy_half(one, at), lambda: copy_half(other, at))

        either(
            other_right,
            n_right == 1,
            lambda: copy_tile(right_tile, rights[0], b * BS),
            lambda: copy_tile(right_tile, rights[-1], b * BS),
        )
        left_high_part, left_low_part = split(left_tile[...])
        right_high_part, right_low_part = split(right_tile[...])
        lhs = jnp.concatenate([left_high_part, left_low_part], axis=1)
        both = jnp.concatenate([right_high_part, right_low_part], axis=1)
        rhs = jnp.concatenate([both, both], axis=0)
        pair = jnp.dot(lhs, rhs, preferred_element_type=jnp.float32)
        place = pl.ds(pl.multiple_of(c * BS, BS), BS)
        total[place, :] = total[place, :] + (pair[:, :BS] + pair[:, BS:])
        return carry

    lax.fori_loop(0, count, body, 0)


WHOLE = ((0, 0), (0, LEFT_HALF))
SMEM_SPEC = pl.BlockSpec(memory_space=pltpu.SMEM)
VMEM_SPEC = pl.BlockSpec(memory_space=pltpu.VMEM)


def step_call(name, sides, out_rows, out_cols, lefts, picks, rights, before=None, flops=10**8):
    operands = [sides, out_rows, out_cols, *lefts, *rights] + ([] if before is None else [before])
    return pl.pallas_call(
        functools.partial(step_kernel, picks, len(lefts), len(rights), before is None),
        out_shape=jax.ShapeDtypeStruct((CMAX * BS, BS), jnp.float32),
        in_specs=[SMEM_SPEC] * 3 + [VMEM_SPEC] * (len(operands) - 3),
        out_specs=VMEM_SPEC,
        input_output_aliases={} if before is None else {len(operands) - 1: 0},
        scratch_shapes=[
            pltpu.VMEM((BS, BS), jnp.float32),
            pltpu.VMEM((BS, BS), jnp.float32),
            pltpu.SMEM((PAD, BS), jnp.float32),
            pltpu.SMEM((PAD, BS), jnp.float32),
            pltpu.SMEM((ROWB * COLB,), jnp.int32),
            pltpu.SMEM((2 * INB + 8,), jnp.int32),
            pltpu.SMEM((32,), jnp.int32),
            pltpu.SemaphoreType.DMA((2,)),
        ],
        compiler_params=pltpu.CompilerParams(vmem_limit_bytes=24 * 2**20),
        cost_estimate=pl.CostEstimate(flops=flops, bytes_accessed=10**6, transcendentals=0),
        name=name,
    )(*operands)


def meta_rows(*parts):
    line = jnp.concatenate(parts).astype(jnp.float32)
    return jnp.pad(line[None], ((0, PAD - 1), (0, BS - line.shape[0])))


def shards(
    left_blocks,
    left_rows,
    left_cols,
    left_count,
    right_blocks,
    right_rows,
    right_cols,
    right_count,
    out_rows,
    out_cols,
):
    left_meta = meta_rows(left_rows[0, 0], left_cols[0, 0], left_count[0])
    right_meta = meta_rows(right_rows[0, 0], right_cols[0, 0], right_count[0])
    blocks = left_blocks.reshape(MAXA * BS, BS)
    low = jnp.concatenate([blocks[:HALF], left_meta])
    high = jnp.concatenate([blocks[HALF:], left_meta])
    left = jnp.concatenate([low, high])
    right = jnp.concatenate([right_blocks.reshape(RIGHT_ROWS, BS), right_meta])
    x = lax.axis_index("col") % GROUP
    row = lax.axis_index("row")
    core = row % 2
    last_chip = (row // 2 == N_ROW // 2 - 1).astype(jnp.int32)
    rows, cols = out_rows[0, 0], out_cols[0, 0]

    high_far = send(high, along_x({0: 3, 1: 2, 2: 0, 3: 1}))
    high_far = send(high, along_x({0: 3, 1: 2, 2: 0, 3: 1}))
    right_near = send(right, route(lambda r, g, x: (r - 2, g, x) if r >= 2 else None))
    right_wrap = send(right, route(lambda r, g, x: (r - 2, g, x) if r < 2 else None))
    near = send(left, along_x({1: 0, 2: 1, 3: 2}))
    low_far = send(low, route(lambda r, g, x: (r, g - 1, x + 2) if x < 2 else (r, g, x - 2)))
    across_high = send(high_far, to_previous_group({3: 2, 2: 3}))
    left, right, high_far = lax.optimization_barrier((left, right, high_far))
    over_low = send(low_far, along_x({2: 3}))
    left, across_high, low_far = lax.optimization_barrier((left, across_high, low_far))
    over_high = send(across_high, along_x({2: 3}))
    total = step_call("step_0", jnp.zeros((2,), jnp.int32), rows, cols, [left], (WHOLE, WHOLE), [right], flops=10000000000)
    right_near, total, near = lax.optimization_barrier((right_near, total, near))
    right_one = send(
        lax.select(core == 1, right, right_near),
        route(lambda r, g, x: (r ^ 1, g, x)),
    )
    right_wrap, over_low, over_high, total = lax.optimization_barrier((right_wrap, over_low, over_high, total))
    edge = send(right_wrap, route(lambda r, g, x: (r + 1, g, x) if r == N_ROW - 2 else None))
    total = step_call(
        "step_2",
        jnp.stack([(x >= 2).astype(jnp.int32), last_chip]),
        rows,
        cols,
        [low_far, high_far, across_high],
        (((0, 0), (1, 0)), ((0, 0), (2, 0))),
        [right_near, right_wrap],
        total,
    )
    total = step_call(
        "step_1",
        jnp.stack([(x == 3).astype(jnp.int32), last_chip * core]),
        rows,
        cols,
        [near, over_low, over_high],
        (WHOLE, ((1, 0), (2, 0))),
        [right_one, edge],
        total,
    )
    return total.reshape(1, 1, CMAX, BS, BS)


def solution(mesh):
    in_specs = (
        P("row", "col", None, None, None),
        P("row", "col", None),
        P("row", "col", None),
        P("row", "col"),
        P("row", "col", None, None, None),
        P("row", "col", None),
        P("row", "col", None),
        P("row", "col"),
        P("row", "col", None),
        P("row", "col", None),
    )
    out_specs = P("row", "col", None, None, None)
    return jax.shard_map(shards, mesh=mesh, in_specs=in_specs, out_specs=out_specs, check_vma=False)
```

```python
import functools

import jax
import jax.numpy as jnp
from jax import lax
from jax.experimental import pallas as pl
from jax.experimental.pallas import tpu as pltpu
from jax.sharding import PartitionSpec as P

BS = 128
MAXA = 8
MAXB = 20
CMAX = 24
ROWB = 8
INB = 32
COLB = 32
HALF = MAXA // 2 * BS
PAD = 8
LEFT_HALF = HALF + PAD
RIGHT_ROWS = MAXB * BS
N_ROW = 32
N_COL = 32
AXES = ("row", "col")

GROUP = 4
N_GROUP = N_COL // GROUP


def route(place):
    pairs = []
    for row in range(N_ROW):
        for col in range(N_COL):
            target = place(row, col // GROUP, col % GROUP)
            if target is not None:
                r, g, x = target
                pairs.append((row * N_COL + col, (r % N_ROW) * N_COL + (g % N_GROUP) * GROUP + x))
    return pairs


def along_x(moves):
    return route(lambda r, g, x: (r, g, moves[x]) if x in moves else None)


def to_previous_group(moves):
    return route(lambda r, g, x: (r, g - 1, moves[x]) if x in moves else None)


def send(block, pairs):
    return lax.ppermute(block, AXES, pairs)


def clear(table, size):
    def body(i, carry):
        table[i] = -1
        return carry

    lax.fori_loop(0, size, body, 0, unroll=8)


def mark_slots(out_rows, out_cols, slot_of):
    clear(slot_of, ROWB * COLB)
    for c in range(CMAX):
        slot_of[out_rows[c] * COLB + out_cols[c]] = c


def list_products(left_meta, right_meta, slot_of, by_inner, products, start):
    def left_int(i):
        return left_meta[0, i].astype(jnp.int32)

    def right_int(i):
        return right_meta[0, i].astype(jnp.int32)

    left_count = left_int(2 * MAXA)
    right_count = right_int(2 * MAXB)
    clear(by_inner, 2 * INB)
    for b in range(MAXB):
        place = jnp.where(b < right_count, right_int(b) * 2, 2 * INB)
        taken = (by_inner[place] >= 0) & (b < right_count)
        by_inner[place + taken.astype(jnp.int32)] = b
    count = start
    for a in range(MAXA):
        row, inner = left_int(a), left_int(MAXA + a)
        for m in range(2):
            b = by_inner[inner * 2 + m]
            column = right_int(MAXB + jnp.maximum(b, 0))
            c = slot_of[row * COLB + column]
            products[count] = (a * 32 + b) * 32 + c
            valid = (a < left_count) & (b >= 0) & (c >= 0)
            count = count + valid.astype(jnp.int32)
    return count


def split(value):
    high = value.astype(jnp.bfloat16)
    low = (value - high.astype(jnp.float32)).astype(jnp.bfloat16)
    return high, low


def step_kernel(passes, n_arrays, first, *refs):
    flags, out_rows, out_cols = refs[:3]
    arrays = refs[3 : 3 + n_arrays]
    (total, left_tile, right_tile, left_meta, right_meta, slot_of, by_inner, products, sems) = refs[-9:]

    def either(flag, no, yes):
        if flag is None:
            no()
        else:
            pl.when(flags[flag] == 0)(no)
            pl.when(flags[flag] == 1)(yes)

    def left_copy(half):
        place, row = half
        return pltpu.make_async_copy(arrays[place].at[pl.ds(row + HALF, PAD)], left_meta, sems.at[0])

    def right_copy(place):
        return pltpu.make_async_copy(arrays[place].at[pl.ds(RIGHT_ROWS, PAD)], right_meta, sems.at[1])

    def start_metas(left_flag, right_flag, lefts, rights):
        either(left_flag, lambda: left_copy(lefts[0][0]).start(), lambda: left_copy(lefts[1][0]).start())
        either(right_flag, lambda: right_copy(rights[0]).start(), lambda: right_copy(rights[1]).start())

    def finish(left_flag, right_flag, lefts, rights):
        left_copy(lefts[0][0]).wait()
        right_copy(rights[0]).wait()
        count = list_products(left_meta, right_meta, slot_of, by_inner, products, 0)

        def copy_tile(tile, place, start):
            tile[...] = arrays[place][pl.ds(pl.multiple_of(start, 8), BS), :]

        def copy_half(half, start):
            copy_tile(left_tile, half[0], half[1] + start)

        def body(i, carry):
            code = products[i]
            a = code // 1024
            b = (code // 32) % 32
            c = code % 32
            upper = a // (MAXA // 2)
            at = (a % (MAXA // 2)) * BS
            for half in range(2):

                @pl.when(upper == half)
                def _():
                    one, other = lefts[0][half], lefts[1][half]
                    flag = None if one == other else left_flag
                    either(flag, lambda: copy_half(one, at), lambda: copy_half(other, at))

            either(
                right_flag,
                lambda: copy_tile(right_tile, rights[0], b * BS),
                lambda: copy_tile(right_tile, rights[1], b * BS),
            )
            left_high_part, left_low_part = split(left_tile[...])
            right_high_part, right_low_part = split(right_tile[...])
            lhs = jnp.concatenate([left_high_part, left_low_part], axis=1)
            both = jnp.concatenate([right_high_part, right_low_part], axis=1)
            rhs = jnp.concatenate([both, both], axis=0)
            pair = jnp.dot(lhs, rhs, preferred_element_type=jnp.float32)
            place = pl.ds(pl.multiple_of(c * BS, BS), BS)
            total[place, :] = total[place, :] + (pair[:, :BS] + pair[:, BS:])
            return carry

        lax.fori_loop(0, count, body, 0)

    def run(index, prepare):
        left_flag, right_flag, enable, lefts, rights = passes[index]

        def whole():
            start_metas(left_flag, right_flag, lefts, rights)
            prepare()
            finish(left_flag, right_flag, lefts, rights)

        if enable is None:
            whole()
        else:
            pl.when(flags[enable] == 1)(whole)

    def prepare():
        mark_slots(out_rows, out_cols, slot_of)
        total[...] = jnp.zeros_like(total) if first else refs[3 + n_arrays][...]

    if passes[0][2] is None:
        run(0, prepare)
    else:
        prepare()
        run(0, lambda: None)
    for index in range(1, len(passes)):
        run(index, lambda: None)


WHOLE = ((0, 0), (0, LEFT_HALF))
SMEM_SPEC = pl.BlockSpec(memory_space=pltpu.SMEM)
VMEM_SPEC = pl.BlockSpec(memory_space=pltpu.VMEM)


def step_call(name, flags, out_rows, out_cols, arrays, passes, before=None, flops=10**8):
    operands = [flags, out_rows, out_cols, *arrays] + ([] if before is None else [before])
    return pl.pallas_call(
        functools.partial(step_kernel, passes, len(arrays), before is None),
        out_shape=jax.ShapeDtypeStruct((CMAX * BS, BS), jnp.float32),
        in_specs=[SMEM_SPEC] * 3 + [VMEM_SPEC] * (len(operands) - 3),
        out_specs=VMEM_SPEC,
        input_output_aliases={} if before is None else {len(operands) - 1: 0},
        scratch_shapes=[
            pltpu.VMEM((BS, BS), jnp.float32),
            pltpu.VMEM((BS, BS), jnp.float32),
            pltpu.SMEM((PAD, BS), jnp.float32),
            pltpu.SMEM((PAD, BS), jnp.float32),
            pltpu.SMEM((ROWB * COLB,), jnp.int32),
            pltpu.SMEM((2 * INB + 8,), jnp.int32),
            pltpu.SMEM((32,), jnp.int32),
            pltpu.SemaphoreType.DMA((2,)),
        ],
        compiler_params=pltpu.CompilerParams(vmem_limit_bytes=24 * 2**20),
        cost_estimate=pl.CostEstimate(flops=flops, bytes_accessed=10**6, transcendentals=0),
        name=name,
    )(*operands)


def meta_rows(*parts):
    line = jnp.concatenate(parts).astype(jnp.float32)
    return jnp.pad(line[None], ((0, PAD - 1), (0, BS - line.shape[0])))


def shards(
    left_blocks,
    left_rows,
    left_cols,
    left_count,
    right_blocks,
    right_rows,
    right_cols,
    right_count,
    out_rows,
    out_cols,
):
    left_meta = meta_rows(left_rows[0, 0], left_cols[0, 0], left_count[0])
    right_meta = meta_rows(right_rows[0, 0], right_cols[0, 0], right_count[0])
    blocks = left_blocks.reshape(MAXA * BS, BS)
    low = jnp.concatenate([blocks[:HALF], left_meta])
    high = jnp.concatenate([blocks[HALF:], left_meta])
    left = jnp.concatenate([low, high])
    right = jnp.concatenate([right_blocks.reshape(RIGHT_ROWS, BS), right_meta])
    x = lax.axis_index("col") % GROUP
    row = lax.axis_index("row")
    core = row % 2
    last_chip = row // 2 == N_ROW // 2 - 1
    rows, cols = out_rows[0, 0], out_cols[0, 0]

    flags = jnp.stack([x == 3, (core == 1) & last_chip, x >= 2, last_chip, ~last_chip]).astype(jnp.int32)
    high_far = send(high, along_x({0: 3, 1: 2, 2: 0, 3: 1}))
    right_near = send(right, route(lambda r, g, x: (r - 2, g, x) if r >= 2 else None))
    low_far = send(low, route(lambda r, g, x: (r, g - 1, x + 2) if x < 2 else (r, g, x - 2)))
    across_high = send(high_far, to_previous_group({3: 2, 2: 3}))
    left, right, high_far = lax.optimization_barrier((left, right, high_far))
    right_wrap = send(right, route(lambda r, g, x: (r - 2, g, x) if r < 2 else None))
    near = send(left, along_x({1: 0, 2: 1, 3: 2}))
    total = step_call("step_0", flags, rows, cols, [left, right], ((None, None, None, (WHOLE, WHOLE), (1, 1)),), flops=2000000000)
    low_far, total = lax.optimization_barrier((low_far, total))
    over_low = send(low_far, along_x({2: 3}))
    across_high, low_far = lax.optimization_barrier((across_high, low_far))
    over_high = send(across_high, along_x({2: 3}))
    right_near, total, across_high = lax.optimization_barrier((right_near, total, across_high))
    right_one = send(
        lax.select(core == 1, right, right_near),
        route(lambda r, g, x: (r ^ 1, g, x)),
    )
    total = step_call(
        "step_2",
        flags,
        rows,
        cols,
        [low_far, high_far, across_high, right_near],
        ((2, None, 4, (((0, 0), (1, 0)), ((0, 0), (2, 0))), (3, 3)),),
        total,
        flops=10000000000,
    )
    right_wrap, over_low, over_high, total, near = lax.optimization_barrier((right_wrap, over_low, over_high, total, near))
    edge = send(right_wrap, route(lambda r, g, x: (r + 1, g, x) if r == N_ROW - 2 else None))
    total = step_call(
        "step_1",
        flags,
        rows,
        cols,
        [near, over_low, over_high, right_one, edge, low_far, high_far, across_high, right_wrap],
        (
            (0, 1, None, (((0, 0), (0, LEFT_HALF)), ((1, 0), (2, 0))), (3, 4)),
            (2, None, 3, (((5, 0), (6, 0)), ((5, 0), (7, 0))), (8, 8)),
        ),
        total,
    )
    return total.reshape(1, 1, CMAX, BS, BS)


def solution(mesh):
    in_specs = (
        P("row", "col", None, None, None),
        P("row", "col", None),
        P("row", "col", None),
        P("row", "col"),
        P("row", "col", None, None, None),
        P("row", "col", None),
        P("row", "col", None),
        P("row", "col"),
        P("row", "col", None),
        P("row", "col", None),
    )
    out_specs = P("row", "col", None, None, None)
    return jax.shard_map(shards, mesh=mesh, in_specs=in_specs, out_specs=out_specs, check_vma=False)
```

```python
import functools

import jax
import jax.numpy as jnp
from jax import lax
from jax.experimental import pallas as pl
from jax.experimental.pallas import tpu as pltpu
from jax.sharding import PartitionSpec as P

BS = 128
MAXA = 8
BATCH = 4
MAXB = 20
CMAX = 24
ROWB = 8
INB = 32
COLB = 32
HALF = MAXA // 2 * BS
PAD = 8
LEFT_HALF = HALF + PAD
RIGHT_ROWS = MAXB * BS
N_ROW = 32
N_COL = 32
AXES = ("row", "col")

GROUP = 4
N_GROUP = N_COL // GROUP


def route(place):
    pairs = []
    for row in range(N_ROW):
        for col in range(N_COL):
            target = place(row, col // GROUP, col % GROUP)
            if target is not None:
                r, g, x = target
                pairs.append((row * N_COL + col, (r % N_ROW) * N_COL + (g % N_GROUP) * GROUP + x))
    return pairs


def along_x(moves):
    return route(lambda r, g, x: (r, g, moves[x]) if x in moves else None)


def to_previous_group(moves):
    return route(lambda r, g, x: (r, g - 1, moves[x]) if x in moves else None)


def send(block, pairs):
    return lax.ppermute(block, AXES, pairs)


def clear(table, size):
    def body(i, carry):
        table[i] = -1
        return carry

    lax.fori_loop(0, size, body, 0, unroll=8)


def mark_slots(out_rows, out_cols, slot_of):
    clear(slot_of, ROWB * COLB)
    for c in range(CMAX):
        slot_of[out_rows[c] * COLB + out_cols[c]] = c


def list_products(left_meta, right_meta, slot_of, by_inner, products, start):
    def left_int(i):
        return left_meta[0, i].astype(jnp.int32)

    def right_int(i):
        return right_meta[0, i].astype(jnp.int32)

    left_count = left_int(2 * MAXA)
    right_count = right_int(2 * MAXB)
    clear(by_inner, 2 * INB)
    for b in range(MAXB):
        place = jnp.where(b < right_count, right_int(b) * 2, 2 * INB)
        taken = (by_inner[place] >= 0) & (b < right_count)
        by_inner[place + taken.astype(jnp.int32)] = b
    count = start
    for a in range(MAXA):
        row, inner = left_int(a), left_int(MAXA + a)
        for m in range(2):
            b = by_inner[inner * 2 + m]
            column = right_int(MAXB + jnp.maximum(b, 0))
            c = slot_of[row * COLB + column]
            products[count] = (a * 32 + b) * 32 + c
            valid = (a < left_count) & (b >= 0) & (c >= 0)
            count = count + valid.astype(jnp.int32)
    return count


def split(value):
    high = value.astype(jnp.bfloat16)
    low = (value - high.astype(jnp.float32)).astype(jnp.bfloat16)
    return high, low


def step_kernel(passes, n_arrays, first, *refs):
    flags, out_rows, out_cols = refs[:3]
    arrays = refs[3 : 3 + n_arrays]
    (total, left_tile, right_tile, left_meta, right_meta, slot_of, by_inner, products, sems) = refs[-9:]

    def either(flag, no, yes):
        if flag is None:
            no()
        else:
            pl.when(flags[flag] == 0)(no)
            pl.when(flags[flag] == 1)(yes)

    def left_copy(half):
        place, row = half
        return pltpu.make_async_copy(arrays[place].at[pl.ds(row + HALF, PAD)], left_meta, sems.at[0])

    def right_copy(place):
        return pltpu.make_async_copy(arrays[place].at[pl.ds(RIGHT_ROWS, PAD)], right_meta, sems.at[1])

    def start_metas(left_flag, right_flag, lefts, rights):
        either(left_flag, lambda: left_copy(lefts[0][0]).start(), lambda: left_copy(lefts[1][0]).start())
        either(right_flag, lambda: right_copy(rights[0]).start(), lambda: right_copy(rights[1]).start())

    def finish(left_flag, right_flag, lefts, rights):
        left_copy(lefts[0][0]).wait()
        right_copy(rights[0]).wait()
        count = list_products(left_meta, right_meta, slot_of, by_inner, products, 0)

        def copy_tile(tile, place, start):
            tile[...] = arrays[place][pl.ds(pl.multiple_of(start, 8), BS), :]

        def body(i, carry):
            codes = [products[i * BATCH + k] for k in range(BATCH)]
            for k, code in enumerate(codes):
                a = code // 1024
                b = (code // 32) % 32
                upper = a // (MAXA // 2)
                at = (a % (MAXA // 2)) * BS
                for half in range(2):

                    def copy_half(source, at=at, k=k):
                        copy_tile(left_tile.at[k], source[0], source[1] + at)

                    @pl.when(upper == half)
                    def _(half=half, copy_half=copy_half):
                        one, other = lefts[0][half], lefts[1][half]
                        flag = None if one == other else left_flag
                        either(flag, lambda: copy_half(one), lambda: copy_half(other))

                either(
                    right_flag,
                    lambda b=b, k=k: copy_tile(right_tile.at[k], rights[0], b * BS),
                    lambda b=b, k=k: copy_tile(right_tile.at[k], rights[1], b * BS),
                )
            values = []
            for k in range(BATCH):
                left_high_part, left_low_part = split(left_tile[k])
                right_high_part, right_low_part = split(right_tile[k])
                lhs = jnp.concatenate([left_high_part, left_low_part], axis=1)
                both = jnp.concatenate([right_high_part, right_low_part], axis=1)
                rhs = jnp.concatenate([both, both], axis=0)
                pair = jnp.dot(lhs, rhs, preferred_element_type=jnp.float32)
                values.append(pair[:, :BS] + pair[:, BS:])
            for k, (code, value) in enumerate(zip(codes, values)):
                place = pl.ds(pl.multiple_of((code % 32) * BS, BS), BS)
                if k > 0:
                    value = jnp.where(i * BATCH + k < count, value, 0.0)
                total[place, :] = total[place, :] + value
            return carry

        for k in range(BATCH - 1):
            products[count + k] = 0
        lax.fori_loop(0, (count + BATCH - 1) // BATCH, body, 0)

    def run(index, prepare):
        left_flag, right_flag, enable, lefts, rights = passes[index]

        def whole():
            start_metas(left_flag, right_flag, lefts, rights)
            prepare()
            finish(left_flag, right_flag, lefts, rights)

        if enable is None:
            whole()
        else:
            pl.when(flags[enable] == 1)(whole)

    def prepare():
        mark_slots(out_rows, out_cols, slot_of)
        total[...] = jnp.zeros_like(total) if first else refs[3 + n_arrays][...]

    if passes[0][2] is None:
        run(0, prepare)
    else:
        prepare()
        run(0, lambda: None)
    for index in range(1, len(passes)):
        run(index, lambda: None)


WHOLE = ((0, 0), (0, LEFT_HALF))
SMEM_SPEC = pl.BlockSpec(memory_space=pltpu.SMEM)
VMEM_SPEC = pl.BlockSpec(memory_space=pltpu.VMEM)


def step_call(name, flags, out_rows, out_cols, arrays, passes, before=None, flops=10**8):
    operands = [flags, out_rows, out_cols, *arrays] + ([] if before is None else [before])
    return pl.pallas_call(
        functools.partial(step_kernel, passes, len(arrays), before is None),
        out_shape=jax.ShapeDtypeStruct((CMAX * BS, BS), jnp.float32),
        in_specs=[SMEM_SPEC] * 3 + [VMEM_SPEC] * (len(operands) - 3),
        out_specs=VMEM_SPEC,
        input_output_aliases={} if before is None else {len(operands) - 1: 0},
        scratch_shapes=[
            pltpu.VMEM((BATCH, BS, BS), jnp.float32),
            pltpu.VMEM((BATCH, BS, BS), jnp.float32),
            pltpu.SMEM((PAD, BS), jnp.float32),
            pltpu.SMEM((PAD, BS), jnp.float32),
            pltpu.SMEM((ROWB * COLB,), jnp.int32),
            pltpu.SMEM((2 * INB + 8,), jnp.int32),
            pltpu.SMEM((32,), jnp.int32),
            pltpu.SemaphoreType.DMA((2,)),
        ],
        compiler_params=pltpu.CompilerParams(vmem_limit_bytes=24 * 2**20),
        cost_estimate=pl.CostEstimate(flops=flops, bytes_accessed=10**6, transcendentals=0),
        name=name,
    )(*operands)


def meta_rows(*parts):
    line = jnp.concatenate(parts).astype(jnp.float32)
    return jnp.pad(line[None], ((0, PAD - 1), (0, BS - line.shape[0])))


def shards(
    left_blocks,
    left_rows,
    left_cols,
    left_count,
    right_blocks,
    right_rows,
    right_cols,
    right_count,
    out_rows,
    out_cols,
):
    left_meta = meta_rows(left_rows[0, 0], left_cols[0, 0], left_count[0])
    right_meta = meta_rows(right_rows[0, 0], right_cols[0, 0], right_count[0])
    blocks = left_blocks.reshape(MAXA * BS, BS)
    low = jnp.concatenate([blocks[:HALF], left_meta])
    high = jnp.concatenate([blocks[HALF:], left_meta])
    left = jnp.concatenate([low, high])
    right = jnp.concatenate([right_blocks.reshape(RIGHT_ROWS, BS), right_meta])
    x = lax.axis_index("col") % GROUP
    row = lax.axis_index("row")
    core = row % 2
    last_chip = row // 2 == N_ROW // 2 - 1
    rows, cols = out_rows[0, 0], out_cols[0, 0]

    flags = jnp.stack([x == 3, (core == 1) & last_chip, x >= 2, last_chip, ~last_chip]).astype(jnp.int32)
    high_far = send(high, along_x({0: 3, 1: 2, 2: 0, 3: 1}))
    right_near = send(right, route(lambda r, g, x: (r - 2, g, x) if r >= 2 else None))
    low_far = send(low, route(lambda r, g, x: (r, g - 1, x + 2) if x < 2 else (r, g, x - 2)))
    across_high = send(high_far, to_previous_group({3: 2, 2: 3}))
    left, right, high_far = lax.optimization_barrier((left, right, high_far))
    right_wrap = send(right, route(lambda r, g, x: (r - 2, g, x) if r < 2 else None))
    near = send(left, along_x({1: 0, 2: 1, 3: 2}))
    over_low = send(low_far, along_x({2: 3}))
    left, across_high, low_far = lax.optimization_barrier((left, across_high, low_far))
    over_high = send(across_high, along_x({2: 3}))
    total = step_call("step_0", flags, rows, cols, [left, right], ((None, None, None, (WHOLE, WHOLE), (1, 1)),), flops=10000000000)
    right_near, total = lax.optimization_barrier((right_near, total))
    right_one = send(
        lax.select(core == 1, right, right_near),
        route(lambda r, g, x: (r ^ 1, g, x)),
    )
    total = step_call(
        "step_2",
        flags,
        rows,
        cols,
        [low_far, high_far, across_high, right_near],
        ((2, None, 4, (((0, 0), (1, 0)), ((0, 0), (2, 0))), (3, 3)),),
        total,
        flops=10000000000,
    )
    right_wrap, over_low, over_high, total, near = lax.optimization_barrier((right_wrap, over_low, over_high, total, near))
    edge = send(right_wrap, route(lambda r, g, x: (r + 1, g, x) if r == N_ROW - 2 else None))
    total = step_call(
        "step_1",
        flags,
        rows,
        cols,
        [near, over_low, over_high, right_one, edge, low_far, high_far, across_high, right_wrap],
        (
            (0, 1, None, (((0, 0), (0, LEFT_HALF)), ((1, 0), (2, 0))), (3, 4)),
            (2, None, 3, (((5, 0), (6, 0)), ((5, 0), (7, 0))), (8, 8)),
        ),
        total,
    )
    return total.reshape(1, 1, CMAX, BS, BS)


def solution(mesh):
    in_specs = (
        P("row", "col", None, None, None),
        P("row", "col", None),
        P("row", "col", None),
        P("row", "col"),
        P("row", "col", None, None, None),
        P("row", "col", None),
        P("row", "col", None),
        P("row", "col"),
        P("row", "col", None),
        P("row", "col", None),
    )
    out_specs = P("row", "col", None, None, None)
    return jax.shard_map(shards, mesh=mesh, in_specs=in_specs, out_specs=out_specs, check_vma=False)
```

```python
import functools

import jax
import jax.numpy as jnp
from jax import lax
from jax.experimental import pallas as pl
from jax.experimental.pallas import tpu as pltpu
from jax.sharding import PartitionSpec as P

BS = 128
MAXA = 8
BATCH = 4
MAXB = 20
CMAX = 24
ROWB = 8
INB = 32
COLB = 32
HALF = MAXA // 2 * BS
PAD = 8
LEFT_HALF = HALF + PAD
RIGHT_ROWS = MAXB * BS
N_ROW = 32
N_COL = 32
AXES = ("row", "col")

GROUP = 4
N_GROUP = N_COL // GROUP


def route(place):
    pairs = []
    for row in range(N_ROW):
        for col in range(N_COL):
            target = place(row, col // GROUP, col % GROUP)
            if target is not None:
                r, g, x = target
                pairs.append((row * N_COL + col, (r % N_ROW) * N_COL + (g % N_GROUP) * GROUP + x))
    return pairs


def along_x(moves):
    return route(lambda r, g, x: (r, g, moves[x]) if x in moves else None)


def to_previous_group(moves):
    return route(lambda r, g, x: (r, g - 1, moves[x]) if x in moves else None)


def send(block, pairs):
    return lax.ppermute(block, AXES, pairs)


def clear(table, size):
    def body(i, carry):
        table[i] = -1
        return carry

    lax.fori_loop(0, size, body, 0, unroll=8)


def mark_slots(out_rows, out_cols, slot_of):
    clear(slot_of, ROWB * COLB)
    for c in range(CMAX):
        slot_of[out_rows[c] * COLB + out_cols[c]] = c


def list_products(left_meta, right_meta, slot_of, by_inner, products, start):
    def left_int(i):
        return left_meta[0, i].astype(jnp.int32)

    def right_int(i):
        return right_meta[0, i].astype(jnp.int32)

    left_count = left_int(2 * MAXA)
    right_count = right_int(2 * MAXB)
    clear(by_inner, 2 * INB)
    for b in range(MAXB):
        place = jnp.where(b < right_count, right_int(b) * 2, 2 * INB)
        taken = (by_inner[place] >= 0) & (b < right_count)
        by_inner[place + taken.astype(jnp.int32)] = b
    count = start
    for a in range(MAXA):
        row, inner = left_int(a), left_int(MAXA + a)
        for m in range(2):
            b = by_inner[inner * 2 + m]
            column = right_int(MAXB + jnp.maximum(b, 0))
            c = slot_of[row * COLB + column]
            products[count] = (a * 32 + b) * 32 + c
            valid = (a < left_count) & (b >= 0) & (c >= 0)
            count = count + valid.astype(jnp.int32)
    return count


def split(value):
    high = value.astype(jnp.bfloat16)
    low = (value - high.astype(jnp.float32)).astype(jnp.bfloat16)
    return high, low


def step_kernel(passes, n_arrays, first, *refs):
    flags, out_rows, out_cols = refs[:3]
    arrays = refs[3 : 3 + n_arrays]
    (total, left_tile, right_tile, left_meta, right_meta, slot_of, by_inner, products, sems) = refs[-9:]

    def either(flag, no, yes):
        if flag is None:
            no()
        else:
            pl.when(flags[flag] == 0)(no)
            pl.when(flags[flag] == 1)(yes)

    def left_copy(half):
        place, row = half
        return pltpu.make_async_copy(arrays[place].at[pl.ds(row + HALF, PAD)], left_meta, sems.at[0])

    def right_copy(place):
        return pltpu.make_async_copy(arrays[place].at[pl.ds(RIGHT_ROWS, PAD)], right_meta, sems.at[1])

    def start_metas(left_flag, right_flag, lefts, rights):
        either(left_flag, lambda: left_copy(lefts[0][0]).start(), lambda: left_copy(lefts[1][0]).start())
        either(right_flag, lambda: right_copy(rights[0]).start(), lambda: right_copy(rights[1]).start())

    def finish(left_flag, right_flag, lefts, rights):
        left_copy(lefts[0][0]).wait()
        right_copy(rights[0]).wait()
        count = list_products(left_meta, right_meta, slot_of, by_inner, products, 0)

        def copy_tile(tile, place, start):
            tile[...] = arrays[place][pl.ds(pl.multiple_of(start, 8), BS), :]

        def body(i, carry):
            codes = [products[i * BATCH + k] for k in range(BATCH)]
            for k, code in enumerate(codes):
                a = code // 1024
                b = (code // 32) % 32
                upper = a // (MAXA // 2)
                at = (a % (MAXA // 2)) * BS
                for half in range(2):

                    def copy_half(source, at=at, k=k):
                        copy_tile(left_tile.at[k], source[0], source[1] + at)

                    @pl.when(upper == half)
                    def _(half=half, copy_half=copy_half):
                        one, other = lefts[0][half], lefts[1][half]
                        flag = None if one == other else left_flag
                        either(flag, lambda: copy_half(one), lambda: copy_half(other))

                either(
                    right_flag,
                    lambda b=b, k=k: copy_tile(right_tile.at[k], rights[0], b * BS),
                    lambda b=b, k=k: copy_tile(right_tile.at[k], rights[1], b * BS),
                )
            values = []
            for k in range(BATCH):
                left_high_part, left_low_part = split(left_tile[k])
                right_high_part, right_low_part = split(right_tile[k])
                lhs = jnp.concatenate([left_high_part, left_low_part], axis=1)
                both = jnp.concatenate([right_high_part, right_low_part], axis=1)
                rhs = jnp.concatenate([both, both], axis=0)
                pair = jnp.dot(lhs, rhs, preferred_element_type=jnp.float32)
                values.append(pair[:, :BS] + pair[:, BS:])
            for k, (code, value) in enumerate(zip(codes, values)):
                place = pl.ds(pl.multiple_of((code % 32) * BS, BS), BS)
                if k > 0:
                    value = jnp.where(i * BATCH + k < count, value, 0.0)
                total[place, :] = total[place, :] + value
            return carry

        for k in range(BATCH - 1):
            products[count + k] = 0
        lax.fori_loop(0, (count + BATCH - 1) // BATCH, body, 0)

    def run(index, prepare):
        left_flag, right_flag, enable, lefts, rights = passes[index]

        def whole():
            start_metas(left_flag, right_flag, lefts, rights)
            prepare()
            finish(left_flag, right_flag, lefts, rights)

        if enable is None:
            whole()
        else:
            pl.when(flags[enable] == 1)(whole)

    def prepare():
        mark_slots(out_rows, out_cols, slot_of)
        total[...] = jnp.zeros_like(total) if first else refs[3 + n_arrays][...]

    if passes[0][2] is None:
        run(0, prepare)
    else:
        prepare()
        run(0, lambda: None)
    for index in range(1, len(passes)):
        run(index, lambda: None)


WHOLE = ((0, 0), (0, LEFT_HALF))
SMEM_SPEC = pl.BlockSpec(memory_space=pltpu.SMEM)
VMEM_SPEC = pl.BlockSpec(memory_space=pltpu.VMEM)


def step_call(name, flags, out_rows, out_cols, arrays, passes, before=None, flops=10**8):
    operands = [flags, out_rows, out_cols, *arrays] + ([] if before is None else [before])
    return pl.pallas_call(
        functools.partial(step_kernel, passes, len(arrays), before is None),
        out_shape=jax.ShapeDtypeStruct((CMAX * BS, BS), jnp.float32),
        in_specs=[SMEM_SPEC] * 3 + [VMEM_SPEC] * (len(operands) - 3),
        out_specs=VMEM_SPEC,
        input_output_aliases={} if before is None else {len(operands) - 1: 0},
        scratch_shapes=[
            pltpu.VMEM((BATCH, BS, BS), jnp.float32),
            pltpu.VMEM((BATCH, BS, BS), jnp.float32),
            pltpu.SMEM((PAD, BS), jnp.float32),
            pltpu.SMEM((PAD, BS), jnp.float32),
            pltpu.SMEM((ROWB * COLB,), jnp.int32),
            pltpu.SMEM((2 * INB + 8,), jnp.int32),
            pltpu.SMEM((32,), jnp.int32),
            pltpu.SemaphoreType.DMA((2,)),
        ],
        compiler_params=pltpu.CompilerParams(vmem_limit_bytes=24 * 2**20),
        cost_estimate=pl.CostEstimate(flops=flops, bytes_accessed=10**6, transcendentals=0),
        name=name,
    )(*operands)


def meta_rows(*parts):
    line = jnp.concatenate(parts).astype(jnp.float32)
    return jnp.pad(line[None], ((0, PAD - 1), (0, BS - line.shape[0])))


def shards(
    left_blocks,
    left_rows,
    left_cols,
    left_count,
    right_blocks,
    right_rows,
    right_cols,
    right_count,
    out_rows,
    out_cols,
):
    left_meta = meta_rows(left_rows[0, 0], left_cols[0, 0], left_count[0])
    right_meta = meta_rows(right_rows[0, 0], right_cols[0, 0], right_count[0])
    blocks = left_blocks.reshape(MAXA * BS, BS)
    low = jnp.concatenate([blocks[:HALF], left_meta])
    high = jnp.concatenate([blocks[HALF:], left_meta])
    left = jnp.concatenate([low, high])
    right = jnp.concatenate([right_blocks.reshape(RIGHT_ROWS, BS), right_meta])
    x = lax.axis_index("col") % GROUP
    row = lax.axis_index("row")
    core = row % 2
    last_chip = row // 2 == N_ROW // 2 - 1
    rows, cols = out_rows[0, 0], out_cols[0, 0]

    flags = jnp.stack([x == 3, (core == 1) & last_chip, x >= 2, last_chip, ~last_chip]).astype(jnp.int32)
    high_far = send(high, along_x({0: 3, 1: 2, 2: 0, 3: 1}))
    right_near = send(right, route(lambda r, g, x: (r - 2, g, x) if r >= 2 else None))
    low_far = send(low, route(lambda r, g, x: (r, g - 1, x + 2) if x < 2 else (r, g, x - 2)))
    across_high = send(high_far, to_previous_group({3: 2, 2: 3}))
    left, right, high_far = lax.optimization_barrier((left, right, high_far))
    left, right, right_near = lax.optimization_barrier((left, right, right_near))
    right_wrap = send(right, route(lambda r, g, x: (r - 2, g, x) if r < 2 else None))
    total = step_call("step_0", flags, rows, cols, [left, right], ((None, None, None, (WHOLE, WHOLE), (1, 1)),), flops=10000000000)
    left, total = lax.optimization_barrier((left, total))
    near = send(left, along_x({1: 0, 2: 1, 3: 2}))
    low_far, total = lax.optimization_barrier((low_far, total))
    over_low = send(low_far, along_x({2: 3}))
    across_high, low_far = lax.optimization_barrier((across_high, low_far))
    over_high = send(across_high, along_x({2: 3}))
    right_one = send(
        lax.select(core == 1, right, right_near),
        route(lambda r, g, x: (r ^ 1, g, x)),
    )
    total = step_call(
        "step_2",
        flags,
        rows,
        cols,
        [low_far, high_far, across_high, right_near],
        ((2, None, 4, (((0, 0), (1, 0)), ((0, 0), (2, 0))), (3, 3)),),
        total,
        flops=3000000000,
    )
    right_wrap, over_low, over_high, total, right_one, near = lax.optimization_barrier((right_wrap, over_low, over_high, total, right_one, near))
    edge = send(right_wrap, route(lambda r, g, x: (r + 1, g, x) if r == N_ROW - 2 else None))
    total = step_call(
        "step_1",
        flags,
        rows,
        cols,
        [near, over_low, over_high, right_one, edge, low_far, high_far, across_high, right_wrap],
        (
            (0, 1, None, (((0, 0), (0, LEFT_HALF)), ((1, 0), (2, 0))), (3, 4)),
            (2, None, 3, (((5, 0), (6, 0)), ((5, 0), (7, 0))), (8, 8)),
        ),
        total,
    )
    return total.reshape(1, 1, CMAX, BS, BS)


def solution(mesh):
    in_specs = (
        P("row", "col", None, None, None),
        P("row", "col", None),
        P("row", "col", None),
        P("row", "col"),
        P("row", "col", None, None, None),
        P("row", "col", None),
        P("row", "col", None),
        P("row", "col"),
        P("row", "col", None),
        P("row", "col", None),
    )
    out_specs = P("row", "col", None, None, None)
    return jax.shard_map(shards, mesh=mesh, in_specs=in_specs, out_specs=out_specs, check_vma=False)
```

```python
import functools

import jax
import jax.numpy as jnp
from jax import lax
from jax.experimental import pallas as pl
from jax.experimental.pallas import tpu as pltpu
from jax.sharding import PartitionSpec as P

BS = 128
MAXA = 8
BATCH = 4
MAXB = 20
CMAX = 24
ROWB = 8
INB = 32
COLB = 32
HALF = MAXA // 2 * BS
PAD = 8
LEFT_HALF = HALF + PAD
RIGHT_ROWS = MAXB * BS
N_ROW = 32
N_COL = 32
AXES = ("row", "col")

GROUP = 4
N_GROUP = N_COL // GROUP


def route(place):
    pairs = []
    for row in range(N_ROW):
        for col in range(N_COL):
            target = place(row, col // GROUP, col % GROUP)
            if target is not None:
                r, g, x = target
                pairs.append((row * N_COL + col, (r % N_ROW) * N_COL + (g % N_GROUP) * GROUP + x))
    return pairs


def ring(row, group, x):
    if row >= 2:
        return row - 2, group, x
    return (N_ROW - 1, group ^ 1, x) if row == 1 else None


def along_x(moves):
    return route(lambda r, g, x: (r, g, moves[x]) if x in moves else None)


def to_previous_group(moves):
    return route(lambda r, g, x: (r, g - 1, moves[x]) if x in moves else None)


def send(block, pairs):
    return lax.ppermute(block, AXES, pairs)


def clear(table, size):
    def body(i, carry):
        table[i] = -1
        return carry

    lax.fori_loop(0, size, body, 0, unroll=8)


def mark_slots(out_rows, out_cols, slot_of):
    clear(slot_of, ROWB * COLB)
    for c in range(CMAX):
        slot_of[out_rows[c] * COLB + out_cols[c]] = c


def list_products(left_meta, right_meta, slot_of, by_inner, products, start):
    def left_int(i):
        return left_meta[0, i].astype(jnp.int32)

    def right_int(i):
        return right_meta[0, i].astype(jnp.int32)

    left_count = left_int(2 * MAXA)
    right_count = right_int(2 * MAXB)
    clear(by_inner, 2 * INB)
    for b in range(MAXB):
        place = jnp.where(b < right_count, right_int(b) * 2, 2 * INB)
        taken = (by_inner[place] >= 0) & (b < right_count)
        by_inner[place + taken.astype(jnp.int32)] = b
    count = start
    for a in range(MAXA):
        row, inner = left_int(a), left_int(MAXA + a)
        for m in range(2):
            b = by_inner[inner * 2 + m]
            column = right_int(MAXB + jnp.maximum(b, 0))
            c = slot_of[row * COLB + column]
            products[count] = (a * 32 + b) * 32 + c
            valid = (a < left_count) & (b >= 0) & (c >= 0)
            count = count + valid.astype(jnp.int32)
    return count


def split(value):
    high = value.astype(jnp.bfloat16)
    low = (value - high.astype(jnp.float32)).astype(jnp.bfloat16)
    return high, low


def step_kernel(passes, n_arrays, first, *refs):
    flags, out_rows, out_cols = refs[:3]
    arrays = refs[3 : 3 + n_arrays]
    (total, left_tile, right_tile, left_meta, right_meta, slot_of, by_inner, products, sems) = refs[-9:]

    def either(flag, no, yes):
        if flag is None:
            no()
        else:
            pl.when(flags[flag] == 0)(no)
            pl.when(flags[flag] == 1)(yes)

    def left_copy(half):
        place, row = half
        return pltpu.make_async_copy(arrays[place].at[pl.ds(row + HALF, PAD)], left_meta, sems.at[0])

    def right_copy(place):
        return pltpu.make_async_copy(arrays[place].at[pl.ds(RIGHT_ROWS, PAD)], right_meta, sems.at[1])

    def start_metas(left_flag, right_flag, lefts, rights):
        either(left_flag, lambda: left_copy(lefts[0][0]).start(), lambda: left_copy(lefts[1][0]).start())
        either(right_flag, lambda: right_copy(rights[0]).start(), lambda: right_copy(rights[1]).start())

    def finish(left_flag, right_flag, lefts, rights):
        left_copy(lefts[0][0]).wait()
        right_copy(rights[0]).wait()
        count = list_products(left_meta, right_meta, slot_of, by_inner, products, 0)

        def copy_tile(tile, place, start):
            tile[...] = arrays[place][pl.ds(pl.multiple_of(start, 8), BS), :]

        def body(i, carry):
            codes = [products[i * BATCH + k] for k in range(BATCH)]
            for k, code in enumerate(codes):
                a = code // 1024
                b = (code // 32) % 32
                upper = a // (MAXA // 2)
                at = (a % (MAXA // 2)) * BS
                for half in range(2):

                    def copy_half(source, at=at, k=k):
                        copy_tile(left_tile.at[k], source[0], source[1] + at)

                    @pl.when(upper == half)
                    def _(half=half, copy_half=copy_half):
                        one, other = lefts[0][half], lefts[1][half]
                        flag = None if one == other else left_flag
                        either(flag, lambda: copy_half(one), lambda: copy_half(other))

                either(
                    right_flag,
                    lambda b=b, k=k: copy_tile(right_tile.at[k], rights[0], b * BS),
                    lambda b=b, k=k: copy_tile(right_tile.at[k], rights[1], b * BS),
                )
            values = []
            for k in range(BATCH):
                left_high_part, left_low_part = split(left_tile[k])
                right_high_part, right_low_part = split(right_tile[k])
                lhs = jnp.concatenate([left_high_part, left_low_part], axis=1)
                both = jnp.concatenate([right_high_part, right_low_part], axis=1)
                rhs = jnp.concatenate([both, both], axis=0)
                pair = jnp.dot(lhs, rhs, preferred_element_type=jnp.float32)
                values.append(pair[:, :BS] + pair[:, BS:])
            for k, (code, value) in enumerate(zip(codes, values)):
                place = pl.ds(pl.multiple_of((code % 32) * BS, BS), BS)
                if k > 0:
                    value = jnp.where(i * BATCH + k < count, value, 0.0)
                total[place, :] = total[place, :] + value
            return carry

        for k in range(BATCH - 1):
            products[count + k] = 0
        lax.fori_loop(0, (count + BATCH - 1) // BATCH, body, 0)

    def run(index, prepare):
        left_flag, right_flag, enable, lefts, rights = passes[index]

        def whole():
            start_metas(left_flag, right_flag, lefts, rights)
            prepare()
            finish(left_flag, right_flag, lefts, rights)

        if enable is None:
            whole()
        else:
            pl.when(flags[enable] == 1)(whole)

    def prepare():
        mark_slots(out_rows, out_cols, slot_of)
        total[...] = jnp.zeros_like(total) if first else refs[3 + n_arrays][...]

    if passes[0][2] is None:
        run(0, prepare)
    else:
        prepare()
        run(0, lambda: None)
    for index in range(1, len(passes)):
        run(index, lambda: None)


WHOLE = ((0, 0), (0, LEFT_HALF))
SMEM_SPEC = pl.BlockSpec(memory_space=pltpu.SMEM)
VMEM_SPEC = pl.BlockSpec(memory_space=pltpu.VMEM)


def step_call(name, flags, out_rows, out_cols, arrays, passes, before=None, flops=10**8):
    operands = [flags, out_rows, out_cols, *arrays] + ([] if before is None else [before])
    return pl.pallas_call(
        functools.partial(step_kernel, passes, len(arrays), before is None),
        out_shape=jax.ShapeDtypeStruct((CMAX * BS, BS), jnp.float32),
        in_specs=[SMEM_SPEC] * 3 + [VMEM_SPEC] * (len(operands) - 3),
        out_specs=VMEM_SPEC,
        input_output_aliases={} if before is None else {len(operands) - 1: 0},
        scratch_shapes=[
            pltpu.VMEM((BATCH, BS, BS), jnp.float32),
            pltpu.VMEM((BATCH, BS, BS), jnp.float32),
            pltpu.SMEM((PAD, BS), jnp.float32),
            pltpu.SMEM((PAD, BS), jnp.float32),
            pltpu.SMEM((ROWB * COLB,), jnp.int32),
            pltpu.SMEM((2 * INB + 8,), jnp.int32),
            pltpu.SMEM((32,), jnp.int32),
            pltpu.SemaphoreType.DMA((2,)),
        ],
        compiler_params=pltpu.CompilerParams(vmem_limit_bytes=24 * 2**20),
        cost_estimate=pl.CostEstimate(flops=flops, bytes_accessed=10**6, transcendentals=0),
        name=name,
    )(*operands)


def meta_rows(*parts):
    line = jnp.concatenate(parts).astype(jnp.float32)
    return jnp.pad(line[None], ((0, PAD - 1), (0, BS - line.shape[0])))


def shards(
    left_blocks,
    left_rows,
    left_cols,
    left_count,
    right_blocks,
    right_rows,
    right_cols,
    right_count,
    out_rows,
    out_cols,
):
    left_meta = meta_rows(left_rows[0, 0], left_cols[0, 0], left_count[0])
    right_meta = meta_rows(right_rows[0, 0], right_cols[0, 0], right_count[0])
    blocks = left_blocks.reshape(MAXA * BS, BS)
    low = jnp.concatenate([blocks[:HALF], left_meta])
    high = jnp.concatenate([blocks[HALF:], left_meta])
    left = jnp.concatenate([low, high])
    right = jnp.concatenate([right_blocks.reshape(RIGHT_ROWS, BS), right_meta])
    x = lax.axis_index("col") % GROUP
    row = lax.axis_index("row")
    core = row % 2
    last_chip = row // 2 == N_ROW // 2 - 1
    rows, cols = out_rows[0, 0], out_cols[0, 0]

    flags = jnp.stack([x == 3, (core == 1) & last_chip, x >= 2, last_chip, ~last_chip, core == 1]).astype(jnp.int32)
    high_far = send(high, along_x({0: 3, 1: 2, 2: 0, 3: 1}))
    right_near = send(right, route(ring))
    low_far = send(low, route(lambda r, g, x: (r, g - 1, x + 2) if x < 2 else (r, g, x - 2)))
    across_high = send(high_far, to_previous_group({3: 2, 2: 3}))
    left, right, high_far = lax.optimization_barrier((left, right, high_far))
    left, right, right_near = lax.optimization_barrier((left, right, right_near))
    right_wrap = send(right, route(lambda r, g, x: (N_ROW - 2, g, x) if r == 0 else None))
    right_cross = send(right_near, route(lambda r, g, x: (r, g ^ 1, x) if r == N_ROW - 1 else None))
    right_one = send(
        lax.select(core == 1, right, right_near),
        route(lambda r, g, x: (r ^ 1, g, x)),
    )
    total = step_call("step_0", flags, rows, cols, [left, right], ((None, None, None, (WHOLE, WHOLE), (1, 1)),), flops=15000000000)
    left, total, right_one = lax.optimization_barrier((left, total, right_one))
    near = send(left, along_x({1: 0, 2: 1, 3: 2}))
    low_far, total = lax.optimization_barrier((low_far, total))
    over_low = send(low_far, along_x({2: 3}))
    across_high, low_far = lax.optimization_barrier((across_high, low_far))
    over_high = send(across_high, along_x({2: 3}))
    total = step_call(
        "step_2",
        flags,
        rows,
        cols,
        [low_far, high_far, across_high, right_near],
        ((2, None, 4, (((0, 0), (1, 0)), ((0, 0), (2, 0))), (3, 3)),),
        total,
        flops=3000000000,
    )
    right_wrap, over_low, over_high, total, near, right_cross = lax.optimization_barrier((right_wrap, over_low, over_high, total, near, right_cross))
    edge = send(right_wrap, route(lambda r, g, x: (r + 1, g, x) if r == N_ROW - 2 else None))
    total = step_call(
        "step_1",
        flags,
        rows,
        cols,
        [near, over_low, over_high, right_one, edge, low_far, high_far, across_high, right_wrap, right_cross],
        (
            (0, 1, None, (((0, 0), (0, LEFT_HALF)), ((1, 0), (2, 0))), (3, 4)),
            (2, 5, 3, (((5, 0), (6, 0)), ((5, 0), (7, 0))), (8, 9)),
        ),
        total,
    )
    return total.reshape(1, 1, CMAX, BS, BS)


def solution(mesh):
    in_specs = (
        P("row", "col", None, None, None),
        P("row", "col", None),
        P("row", "col", None),
        P("row", "col"),
        P("row", "col", None, None, None),
        P("row", "col", None),
        P("row", "col", None),
        P("row", "col"),
        P("row", "col", None),
        P("row", "col", None),
    )
    out_specs = P("row", "col", None, None, None)
    return jax.shard_map(shards, mesh=mesh, in_specs=in_specs, out_specs=out_specs, check_vma=False)
```

```python
import functools

import jax
import jax.numpy as jnp
from jax import lax
from jax.experimental import pallas as pl
from jax.experimental.pallas import tpu as pltpu
from jax.sharding import PartitionSpec as P

BS = 128
MAXA = 8
BATCH = 4
MAXB = 20
CMAX = 24
ROWB = 8
INB = 32
COLB = 32
HALF = MAXA // 2 * BS
PAD = 8
LEFT_HALF = HALF + PAD
RIGHT_ROWS = MAXB * BS
N_ROW = 32
N_COL = 32
AXES = ("row", "col")

GROUP = 4
N_GROUP = N_COL // GROUP


def route(place):
    pairs = []
    for row in range(N_ROW):
        for col in range(N_COL):
            target = place(row, col // GROUP, col % GROUP)
            if target is not None:
                r, g, x = target
                pairs.append((row * N_COL + col, (r % N_ROW) * N_COL + (g % N_GROUP) * GROUP + x))
    return pairs


def ring(row, group, x):
    if row >= 2:
        return row - 2, group, x
    return (N_ROW - 1, group ^ 1, x) if row == 1 else None


def along_x(moves):
    return route(lambda r, g, x: (r, g, moves[x]) if x in moves else None)


def to_previous_group(moves):
    return route(lambda r, g, x: (r, g - 1, moves[x]) if x in moves else None)


def send(block, pairs):
    return lax.ppermute(block, AXES, pairs)


def clear(table, size):
    def body(i, carry):
        table[i] = -1
        return carry

    lax.fori_loop(0, size, body, 0, unroll=8)


def mark_slots(out_rows, out_cols, slot_of):
    clear(slot_of, ROWB * COLB)
    for c in range(CMAX):
        slot_of[out_rows[c] * COLB + out_cols[c]] = c


def list_products(left_meta, right_meta, slot_of, by_inner, products, start):
    def left_int(i):
        return left_meta[0, i].astype(jnp.int32)

    def right_int(i):
        return right_meta[0, i].astype(jnp.int32)

    left_count = left_int(2 * MAXA)
    right_count = right_int(2 * MAXB)
    clear(by_inner, 2 * INB)
    for b in range(MAXB):
        place = jnp.where(b < right_count, right_int(b) * 2, 2 * INB)
        taken = (by_inner[place] >= 0) & (b < right_count)
        by_inner[place + taken.astype(jnp.int32)] = b
    count = start
    for a in range(MAXA):
        row, inner = left_int(a), left_int(MAXA + a)
        for m in range(2):
            b = by_inner[inner * 2 + m]
            column = right_int(MAXB + jnp.maximum(b, 0))
            c = slot_of[row * COLB + column]
            products[count] = (a * 32 + b) * 32 + c
            valid = (a < left_count) & (b >= 0) & (c >= 0)
            count = count + valid.astype(jnp.int32)
    return count


def split(value):
    high = value.astype(jnp.bfloat16)
    low = (value - high.astype(jnp.float32)).astype(jnp.bfloat16)
    return high, low


def step_kernel(passes, n_arrays, first, *refs):
    flags, out_rows, out_cols = refs[:3]
    arrays = refs[3 : 3 + n_arrays]
    (total, left_tile, right_tile, left_meta, right_meta, slot_of, by_inner, products, sems) = refs[-9:]

    def either(flag, no, yes):
        if flag is None:
            no()
        else:
            pl.when(flags[flag] == 0)(no)
            pl.when(flags[flag] == 1)(yes)

    def left_copy(half):
        place, row = half
        return pltpu.make_async_copy(arrays[place].at[pl.ds(row + HALF, PAD)], left_meta, sems.at[0])

    def right_copy(place):
        return pltpu.make_async_copy(arrays[place].at[pl.ds(RIGHT_ROWS, PAD)], right_meta, sems.at[1])

    def start_metas(left_flag, right_flag, lefts, rights):
        either(left_flag, lambda: left_copy(lefts[0][0]).start(), lambda: left_copy(lefts[1][0]).start())
        either(right_flag, lambda: right_copy(rights[0]).start(), lambda: right_copy(rights[1]).start())

    def finish(left_flag, right_flag, lefts, rights):
        left_copy(lefts[0][0]).wait()
        right_copy(rights[0]).wait()
        count = list_products(left_meta, right_meta, slot_of, by_inner, products, 0)

        def copy_tile(tile, place, start):
            tile[...] = arrays[place][pl.ds(pl.multiple_of(start, 8), BS), :]

        def body(i, carry):
            codes = [products[i * BATCH + k] for k in range(BATCH)]
            for k, code in enumerate(codes):
                a = code // 1024
                b = (code // 32) % 32
                upper = a // (MAXA // 2)
                at = (a % (MAXA // 2)) * BS
                for half in range(2):

                    def copy_half(source, at=at, k=k):
                        copy_tile(left_tile.at[k], source[0], source[1] + at)

                    @pl.when(upper == half)
                    def _(half=half, copy_half=copy_half):
                        one, other = lefts[0][half], lefts[1][half]
                        flag = None if one == other else left_flag
                        either(flag, lambda: copy_half(one), lambda: copy_half(other))

                either(
                    right_flag,
                    lambda b=b, k=k: copy_tile(right_tile.at[k], rights[0], b * BS),
                    lambda b=b, k=k: copy_tile(right_tile.at[k], rights[1], b * BS),
                )
            values = []
            for k in range(BATCH):
                left_high_part, left_low_part = split(left_tile[k])
                right_high_part, right_low_part = split(right_tile[k])
                lhs = jnp.concatenate([left_high_part, left_low_part], axis=1)
                both = jnp.concatenate([right_high_part, right_low_part], axis=1)
                rhs = jnp.concatenate([both, both], axis=0)
                pair = jnp.dot(lhs, rhs, preferred_element_type=jnp.float32)
                values.append(pair[:, :BS] + pair[:, BS:])
            for k, (code, value) in enumerate(zip(codes, values)):
                place = pl.ds(pl.multiple_of((code % 32) * BS, BS), BS)
                if k > 0:
                    value = jnp.where(i * BATCH + k < count, value, 0.0)
                total[place, :] = total[place, :] + value
            return carry

        for k in range(BATCH - 1):
            products[count + k] = 0
        lax.fori_loop(0, (count + BATCH - 1) // BATCH, body, 0)

    def run(index, prepare):
        left_flag, right_flag, enable, lefts, rights = passes[index]

        def whole():
            start_metas(left_flag, right_flag, lefts, rights)
            prepare()
            finish(left_flag, right_flag, lefts, rights)

        if enable is None:
            whole()
        else:
            pl.when(flags[enable] == 1)(whole)

    def prepare():
        mark_slots(out_rows, out_cols, slot_of)
        total[...] = jnp.zeros_like(total) if first else refs[3 + n_arrays][...]

    if passes[0][2] is None:
        run(0, prepare)
    else:
        prepare()
        run(0, lambda: None)
    for index in range(1, len(passes)):
        run(index, lambda: None)


WHOLE = ((0, 0), (0, LEFT_HALF))
SMEM_SPEC = pl.BlockSpec(memory_space=pltpu.SMEM)
VMEM_SPEC = pl.BlockSpec(memory_space=pltpu.VMEM)


def step_call(name, flags, out_rows, out_cols, arrays, passes, before=None, flops=10**8):
    operands = [flags, out_rows, out_cols, *arrays] + ([] if before is None else [before])
    return pl.pallas_call(
        functools.partial(step_kernel, passes, len(arrays), before is None),
        out_shape=jax.ShapeDtypeStruct((CMAX * BS, BS), jnp.float32),
        in_specs=[SMEM_SPEC] * 3 + [VMEM_SPEC] * (len(operands) - 3),
        out_specs=VMEM_SPEC,
        input_output_aliases={} if before is None else {len(operands) - 1: 0},
        scratch_shapes=[
            pltpu.VMEM((BATCH, BS, BS), jnp.float32),
            pltpu.VMEM((BATCH, BS, BS), jnp.float32),
            pltpu.SMEM((PAD, BS), jnp.float32),
            pltpu.SMEM((PAD, BS), jnp.float32),
            pltpu.SMEM((ROWB * COLB,), jnp.int32),
            pltpu.SMEM((2 * INB + 8,), jnp.int32),
            pltpu.SMEM((32,), jnp.int32),
            pltpu.SemaphoreType.DMA((2,)),
        ],
        compiler_params=pltpu.CompilerParams(vmem_limit_bytes=24 * 2**20),
        cost_estimate=pl.CostEstimate(flops=flops, bytes_accessed=10**6, transcendentals=0),
        name=name,
    )(*operands)


def meta_rows(*parts):
    line = jnp.concatenate(parts).astype(jnp.float32)
    return jnp.pad(line[None], ((0, PAD - 1), (0, BS - line.shape[0])))


def shards(
    left_blocks,
    left_rows,
    left_cols,
    left_count,
    right_blocks,
    right_rows,
    right_cols,
    right_count,
    out_rows,
    out_cols,
):
    left_meta = meta_rows(left_rows[0, 0], left_cols[0, 0], left_count[0])
    right_meta = meta_rows(right_rows[0, 0], right_cols[0, 0], right_count[0])
    blocks = left_blocks.reshape(MAXA * BS, BS)
    low = jnp.concatenate([blocks[:HALF], left_meta])
    high = jnp.concatenate([blocks[HALF:], left_meta])
    left = jnp.concatenate([low, high])
    right = jnp.concatenate([right_blocks.reshape(RIGHT_ROWS, BS), right_meta])
    x = lax.axis_index("col") % GROUP
    row = lax.axis_index("row")
    core = row % 2
    last_chip = row // 2 == N_ROW // 2 - 1
    rows, cols = out_rows[0, 0], out_cols[0, 0]

    flags = jnp.stack([x == 3, (core == 1) & last_chip, x >= 2, last_chip, ~last_chip, core == 1]).astype(jnp.int32)
    high_far = send(high, along_x({0: 3, 1: 2, 2: 0, 3: 1}))
    right_near = send(right, route(ring))
    right_wrap = send(right, route(lambda r, g, x: (N_ROW - 2, g, x) if r == 0 else None))
    low_far = send(low, route(lambda r, g, x: (r, g - 1, x + 2) if x < 2 else (r, g, x - 2)))
    across_high = send(high_far, to_previous_group({3: 2, 2: 3}))
    left, right, high_far = lax.optimization_barrier((left, right, high_far))
    left, right, right_near = lax.optimization_barrier((left, right, right_near))
    right_cross = send(right_near, route(lambda r, g, x: (r, g ^ 1, x) if r == N_ROW - 1 else None))
    right_one = send(
        lax.select(core == 1, right, right_near),
        route(lambda r, g, x: (r ^ 1, g, x)),
    )
    total = step_call("step_0", flags, rows, cols, [left, right], ((None, None, None, (WHOLE, WHOLE), (1, 1)),), flops=15000000000)
    left, total, right_one = lax.optimization_barrier((left, total, right_one))
    near = send(left, along_x({1: 0, 2: 1, 3: 2}))
    low_far, total = lax.optimization_barrier((low_far, total))
    over_low = send(low_far, along_x({2: 3}))
    across_high, low_far = lax.optimization_barrier((across_high, low_far))
    over_high = send(across_high, along_x({2: 3}))
    total = step_call(
        "step_2",
        flags,
        rows,
        cols,
        [low_far, high_far, across_high, right_near],
        ((2, None, 4, (((0, 0), (1, 0)), ((0, 0), (2, 0))), (3, 3)),),
        total,
        flops=3000000000,
    )
    right_wrap, over_low, over_high, total, near, right_cross = lax.optimization_barrier((right_wrap, over_low, over_high, total, near, right_cross))
    edge = send(right_wrap, route(lambda r, g, x: (r + 1, g, x) if r == N_ROW - 2 else None))
    total = step_call(
        "step_1",
        flags,
        rows,
        cols,
        [near, over_low, over_high, right_one, edge, low_far, high_far, across_high, right_wrap, right_cross],
        (
            (0, 1, None, (((0, 0), (0, LEFT_HALF)), ((1, 0), (2, 0))), (3, 4)),
            (2, 5, 3, (((5, 0), (6, 0)), ((5, 0), (7, 0))), (8, 9)),
        ),
        total,
    )
    return total.reshape(1, 1, CMAX, BS, BS)


def solution(mesh):
    in_specs = (
        P("row", "col", None, None, None),
        P("row", "col", None),
        P("row", "col", None),
        P("row", "col"),
        P("row", "col", None, None, None),
        P("row", "col", None),
        P("row", "col", None),
        P("row", "col"),
        P("row", "col", None),
        P("row", "col", None),
    )
    out_specs = P("row", "col", None, None, None)
    return jax.shard_map(shards, mesh=mesh, in_specs=in_specs, out_specs=out_specs, check_vma=False)
```

```python
import functools

import jax
import jax.numpy as jnp
from jax import lax
from jax.experimental import pallas as pl
from jax.experimental.pallas import tpu as pltpu
from jax.sharding import PartitionSpec as P

BS = 128
MAXA = 8
BATCH = 4
MAXB = 20
CMAX = 24
ROWB = 8
INB = 32
COLB = 32
HALF = MAXA // 2 * BS
PAD = 8
LEFT_HALF = HALF + PAD
RIGHT_ROWS = MAXB * BS
N_ROW = 32
N_COL = 32
AXES = ("row", "col")

GROUP = 4
N_GROUP = N_COL // GROUP


def route(place):
    pairs = []
    for row in range(N_ROW):
        for col in range(N_COL):
            target = place(row, col // GROUP, col % GROUP)
            if target is not None:
                r, g, x = target
                pairs.append((row * N_COL + col, (r % N_ROW) * N_COL + (g % N_GROUP) * GROUP + x))
    return pairs


def ring(row, group, x):
    if row >= 2:
        return row - 2, group, x
    return (N_ROW - 1, group ^ 1, x) if row == 1 else None


def along_x(moves):
    return route(lambda r, g, x: (r, g, moves[x]) if x in moves else None)


def to_previous_group(moves):
    return route(lambda r, g, x: (r, g - 1, moves[x]) if x in moves else None)


def send(block, pairs):
    return lax.ppermute(block, AXES, pairs)


def clear(table, size):
    def body(i, carry):
        table[i] = -1
        return carry

    lax.fori_loop(0, size, body, 0, unroll=8)


def mark_slots(out_rows, out_cols, slot_of):
    clear(slot_of, ROWB * COLB)
    for c in range(CMAX):
        slot_of[out_rows[c] * COLB + out_cols[c]] = c


def list_products(left_meta, right_meta, slot_of, by_inner, products, start):
    def left_int(i):
        return left_meta[0, i].astype(jnp.int32)

    def right_int(i):
        return right_meta[0, i].astype(jnp.int32)

    left_count = left_int(2 * MAXA)
    right_count = right_int(2 * MAXB)
    clear(by_inner, 2 * INB)
    for b in range(MAXB):
        place = jnp.where(b < right_count, right_int(b) * 2, 2 * INB)
        taken = (by_inner[place] >= 0) & (b < right_count)
        by_inner[place + taken.astype(jnp.int32)] = b
    count = start
    for a in range(MAXA):
        row, inner = left_int(a), left_int(MAXA + a)
        for m in range(2):
            b = by_inner[inner * 2 + m]
            column = right_int(MAXB + jnp.maximum(b, 0))
            c = slot_of[row * COLB + column]
            products[count] = (a * 32 + b) * 32 + c
            valid = (a < left_count) & (b >= 0) & (c >= 0)
            count = count + valid.astype(jnp.int32)
    return count


def split(value):
    high = value.astype(jnp.bfloat16)
    low = (value - high.astype(jnp.float32)).astype(jnp.bfloat16)
    return high, low


def step_kernel(passes, n_arrays, first, *refs):
    flags, out_rows, out_cols = refs[:3]
    arrays = refs[3 : 3 + n_arrays]
    (total, left_tile, right_tile, left_meta, right_meta, slot_of, by_inner, products, sems) = refs[-9:]

    def either(flag, no, yes):
        if flag is None:
            no()
        else:
            pl.when(flags[flag] == 0)(no)
            pl.when(flags[flag] == 1)(yes)

    def left_copy(half):
        place, row = half
        return pltpu.make_async_copy(arrays[place].at[pl.ds(row + HALF, PAD)], left_meta, sems.at[0])

    def right_copy(place):
        return pltpu.make_async_copy(arrays[place].at[pl.ds(RIGHT_ROWS, PAD)], right_meta, sems.at[1])

    def start_metas(left_flag, right_flag, lefts, rights):
        either(left_flag, lambda: left_copy(lefts[0][0]).start(), lambda: left_copy(lefts[1][0]).start())
        either(right_flag, lambda: right_copy(rights[0]).start(), lambda: right_copy(rights[1]).start())

    def finish(left_flag, right_flag, lefts, rights):
        left_copy(lefts[0][0]).wait()
        right_copy(rights[0]).wait()
        count = list_products(left_meta, right_meta, slot_of, by_inner, products, 0)

        def copy_tile(tile, place, start):
            tile[...] = arrays[place][pl.ds(pl.multiple_of(start, 8), BS), :]

        def body(i, carry):
            codes = [products[i * BATCH + k] for k in range(BATCH)]
            for k, code in enumerate(codes):
                a = code // 1024
                b = (code // 32) % 32
                upper = a // (MAXA // 2)
                at = (a % (MAXA // 2)) * BS
                for half in range(2):

                    def copy_half(source, at=at, k=k):
                        copy_tile(left_tile.at[k], source[0], source[1] + at)

                    @pl.when(upper == half)
                    def _(half=half, copy_half=copy_half):
                        one, other = lefts[0][half], lefts[1][half]
                        flag = None if one == other else left_flag
                        either(flag, lambda: copy_half(one), lambda: copy_half(other))

                either(
                    right_flag,
                    lambda b=b, k=k: copy_tile(right_tile.at[k], rights[0], b * BS),
                    lambda b=b, k=k: copy_tile(right_tile.at[k], rights[1], b * BS),
                )
            values = []
            for k in range(BATCH):
                left_high_part, left_low_part = split(left_tile[k])
                right_high_part, right_low_part = split(right_tile[k])
                lhs = jnp.concatenate([left_high_part, left_low_part], axis=1)
                both = jnp.concatenate([right_high_part, right_low_part], axis=1)
                rhs = jnp.concatenate([both, both], axis=0)
                pair = jnp.dot(lhs, rhs, preferred_element_type=jnp.float32)
                values.append(pair[:, :BS] + pair[:, BS:])
            for k, (code, value) in enumerate(zip(codes, values)):
                place = pl.ds(pl.multiple_of((code % 32) * BS, BS), BS)
                if k > 0:
                    value = jnp.where(i * BATCH + k < count, value, 0.0)
                total[place, :] = total[place, :] + value
            return carry

        for k in range(BATCH - 1):
            products[count + k] = 0
        lax.fori_loop(0, (count + BATCH - 1) // BATCH, body, 0)

    def run(index, prepare):
        left_flag, right_flag, enable, lefts, rights = passes[index]

        def whole():
            start_metas(left_flag, right_flag, lefts, rights)
            prepare()
            finish(left_flag, right_flag, lefts, rights)

        if enable is None:
            whole()
        else:
            pl.when(flags[enable] == 1)(whole)

    def prepare():
        mark_slots(out_rows, out_cols, slot_of)
        total[...] = jnp.zeros_like(total) if first else refs[3 + n_arrays][...]

    if passes[0][2] is None:
        run(0, prepare)
    else:
        prepare()
        run(0, lambda: None)
    for index in range(1, len(passes)):
        run(index, lambda: None)


WHOLE = ((0, 0), (0, LEFT_HALF))
SMEM_SPEC = pl.BlockSpec(memory_space=pltpu.SMEM)
VMEM_SPEC = pl.BlockSpec(memory_space=pltpu.VMEM)


def step_call(name, flags, out_rows, out_cols, arrays, passes, before=None, flops=10**8):
    operands = [flags, out_rows, out_cols, *arrays] + ([] if before is None else [before])
    return pl.pallas_call(
        functools.partial(step_kernel, passes, len(arrays), before is None),
        out_shape=jax.ShapeDtypeStruct((CMAX * BS, BS), jnp.float32),
        in_specs=[SMEM_SPEC] * 3 + [VMEM_SPEC] * (len(operands) - 3),
        out_specs=VMEM_SPEC,
        input_output_aliases={} if before is None else {len(operands) - 1: 0},
        scratch_shapes=[
            pltpu.VMEM((BATCH, BS, BS), jnp.float32),
            pltpu.VMEM((BATCH, BS, BS), jnp.float32),
            pltpu.SMEM((PAD, BS), jnp.float32),
            pltpu.SMEM((PAD, BS), jnp.float32),
            pltpu.SMEM((ROWB * COLB,), jnp.int32),
            pltpu.SMEM((2 * INB + 8,), jnp.int32),
            pltpu.SMEM((32,), jnp.int32),
            pltpu.SemaphoreType.DMA((2,)),
        ],
        compiler_params=pltpu.CompilerParams(vmem_limit_bytes=24 * 2**20),
        cost_estimate=pl.CostEstimate(flops=flops, bytes_accessed=10**6, transcendentals=0),
        name=name,
    )(*operands)


def joined(blocks, meta):
    def kernel(blocks_ref, meta_ref, out_ref):
        out_ref[pl.ds(0, RIGHT_ROWS), :] = blocks_ref[...]
        out_ref[pl.ds(RIGHT_ROWS, PAD), :] = meta_ref[...]

    return pl.pallas_call(
        kernel,
        out_shape=jax.ShapeDtypeStruct((RIGHT_ROWS + PAD, BS), jnp.float32),
        in_specs=[VMEM_SPEC] * 2,
        out_specs=VMEM_SPEC,
        compiler_params=pltpu.CompilerParams(vmem_limit_bytes=8 * 2**20),
        name="joined",
    )(blocks, meta)


def meta_rows(*parts):
    line = jnp.concatenate(parts).astype(jnp.float32)
    return jnp.pad(line[None], ((0, PAD - 1), (0, BS - line.shape[0])))


def shards(
    left_blocks,
    left_rows,
    left_cols,
    left_count,
    right_blocks,
    right_rows,
    right_cols,
    right_count,
    out_rows,
    out_cols,
):
    left_meta = meta_rows(left_rows[0, 0], left_cols[0, 0], left_count[0])
    right_meta = meta_rows(right_rows[0, 0], right_cols[0, 0], right_count[0])
    blocks = left_blocks.reshape(MAXA * BS, BS)
    low = jnp.concatenate([blocks[:HALF], left_meta])
    high = jnp.concatenate([blocks[HALF:], left_meta])
    left = jnp.concatenate([low, high])
    right = joined(right_blocks.reshape(RIGHT_ROWS, BS), right_meta)
    x = lax.axis_index("col") % GROUP
    row = lax.axis_index("row")
    core = row % 2
    last_chip = row // 2 == N_ROW // 2 - 1
    rows, cols = out_rows[0, 0], out_cols[0, 0]

    flags = jnp.stack([x == 3, (core == 1) & last_chip, x >= 2, last_chip, ~last_chip, core == 1]).astype(jnp.int32)
    high_far = send(high, along_x({0: 3, 1: 2, 2: 0, 3: 1}))
    right_near = send(right, route(ring))
    low_far = send(low, route(lambda r, g, x: (r, g - 1, x + 2) if x < 2 else (r, g, x - 2)))
    across_high = send(high_far, to_previous_group({3: 2, 2: 3}))
    left, right, high_far = lax.optimization_barrier((left, right, high_far))
    left, right, right_near = lax.optimization_barrier((left, right, right_near))
    right_wrap = send(right, route(lambda r, g, x: (N_ROW - 2, g, x) if r == 0 else None))
    right_cross = send(right_near, route(lambda r, g, x: (r, g ^ 1, x) if r == N_ROW - 1 else None))
    right_one = send(
        lax.select(core == 1, right, right_near),
        route(lambda r, g, x: (r ^ 1, g, x)),
    )
    total = step_call("step_0", flags, rows, cols, [left, right], ((None, None, None, (WHOLE, WHOLE), (1, 1)),), flops=15000000000)
    left, total, right_one = lax.optimization_barrier((left, total, right_one))
    near = send(left, along_x({1: 0, 2: 1, 3: 2}))
    low_far, total = lax.optimization_barrier((low_far, total))
    over_low = send(low_far, along_x({2: 3}))
    across_high, low_far = lax.optimization_barrier((across_high, low_far))
    over_high = send(across_high, along_x({2: 3}))
    total = step_call(
        "step_2",
        flags,
        rows,
        cols,
        [low_far, high_far, across_high, right_near],
        ((2, None, 4, (((0, 0), (1, 0)), ((0, 0), (2, 0))), (3, 3)),),
        total,
        flops=3000000000,
    )
    right_wrap, over_low, over_high, total, near, right_cross = lax.optimization_barrier((right_wrap, over_low, over_high, total, near, right_cross))
    edge = send(right_wrap, route(lambda r, g, x: (r + 1, g, x) if r == N_ROW - 2 else None))
    total = step_call(
        "step_1",
        flags,
        rows,
        cols,
        [near, over_low, over_high, right_one, edge, low_far, high_far, across_high, right_wrap, right_cross],
        (
            (0, 1, None, (((0, 0), (0, LEFT_HALF)), ((1, 0), (2, 0))), (3, 4)),
            (2, 5, 3, (((5, 0), (6, 0)), ((5, 0), (7, 0))), (8, 9)),
        ),
        total,
    )
    return total.reshape(1, 1, CMAX, BS, BS)


def solution(mesh):
    in_specs = (
        P("row", "col", None, None, None),
        P("row", "col", None),
        P("row", "col", None),
        P("row", "col"),
        P("row", "col", None, None, None),
        P("row", "col", None),
        P("row", "col", None),
        P("row", "col"),
        P("row", "col", None),
        P("row", "col", None),
    )
    out_specs = P("row", "col", None, None, None)
    return jax.shard_map(shards, mesh=mesh, in_specs=in_specs, out_specs=out_specs, check_vma=False)
```
